512 devices in a mesh: gx: 32 (over x, z_lo, core), gy: 16 (over y, z_hi).
Axes of the slice: x: 4, y: 4, z: 16 (z_hi: 4, z_lo: 4; z = z_hi * 4 + z_lo), core: 2. Of those that a mesh axis runs over, the one named last changes fastest.
Arguments:
- state_field: float32 [128, 128, 2304], P('gx', 'gy'), may hold values from -6 to 6
- conv_first: float32 [3, 3, 36, 108], replicated, may hold values from -0.1875 to 0.1875
- conv_second: float32 [3, 3, 36, 108], replicated, may hold values from -0.1875 to 0.1875
- spec_real: float32 [32, 32, 36, 432], P('gx', 'gy'), may hold values from -12 to 12
- spec_imag: float32 [32, 32, 36, 432], P('gx', 'gy'), may hold values from -12 to 12
Outputs:
- layer_out: float32 [128, 128, 2304], P('gx', 'gy')
The draws below stay inside these ranges and needn't reach their ends.
All inputs are finite; a program needn't handle non-finite values.
Results may differ from the reference program's by a relative error of at most 0.00007.
Values sent between devices are 32-bit elements; how exact they have to be, the bound alone decides.
A program may use at most 128 MiB of HBM per device.

```python
import jax
import jax.numpy as jnp
from jax import lax

C = 36
Z = 64
MX = 16
MY = 16
MZ = 12
X = 128
Y = 128


def levels(rng, extent, shards, smallest, largest):
    level, own = 1.0, jax.random.fold_in(rng, 6)
    for dim, parts in shards:
        draws = jnp.exp(jax.random.uniform(jax.random.fold_in(own, dim), (parts,), jnp.float32, smallest / len(shards), largest / len(shards)))
        level = level * jnp.repeat(draws, extent[dim] // parts).reshape([-1 if axis == dim else 1 for axis in range(len(extent))])
    return level


def gaussian(own_key, shape, spread, reach, shards=(), held_as=jnp.bfloat16):
    entries = spread * jax.random.normal(own_key, shape, jnp.float32)
    if shards:
        entries = entries * levels(own_key, shape, shards, -0.22, 0.18)
    return jnp.clip(entries, -reach, reach).astype(held_as)


def setup_inputs(seed: int = 0) -> dict:
    seeds = jax.random.split(jax.random.key(seed), 6)
    state_field = gaussian(seeds[0], (X, Y, C * Z), 1.0, 6.0, ((0, 32), (1, 16)), jnp.float32)
    conv_first = gaussian(seeds[1], (3, 3, C, 3 * C), (27 * C) ** -0.5, 0.1875, (), jnp.float32)
    conv_second = gaussian(seeds[2], (3, 3, C, 3 * C), (27 * C) ** -0.5, 0.1875, (), jnp.float32)
    spec_real = gaussian(seeds[3], (2 * MX, 2 * MY, C, MZ * C), 2.0, 12.0, ((0, 32), (1, 16)), jnp.float32)
    spec_imag = gaussian(seeds[4], (2 * MX, 2 * MY, C, MZ * C), 2.0, 12.0, ((0, 32), (1, 16)), jnp.float32)
    return dict(state_field=state_field, conv_first=conv_first, conv_second=conv_second, spec_real=spec_real, spec_imag=spec_imag)


def kept_modes(mode_count, length):
    places = jnp.arange(2 * mode_count, dtype=jnp.int32)
    return jnp.where(places < mode_count, places, places + length - 2 * mode_count).astype(jnp.int32)


def convolve(volume, kernel):
    operand = jnp.transpose(volume, (2, 0, 1, 3))[None]
    filters = jnp.transpose(kernel.reshape(3, 3, C, 3, C), (2, 4, 0, 1, 3))
    result = lax.conv_general_dilated(operand, filters, (1, 1, 1), [(1, 1), (1, 1), (1, 1)], dimension_numbers=("NCDHW", "OIDHW", "NCDHW"), precision=lax.Precision.HIGHEST)
    return jnp.transpose(result[0], (1, 2, 0, 3))


def reference(state_field, conv_first, conv_second, spec_real, spec_imag):
    highest = lax.Precision.HIGHEST
    volume = state_field.reshape(X, Y, C, Z)
    hidden_field = jax.nn.gelu(convolve(volume, conv_first), approximate=False)
    conv_out = convolve(hidden_field, conv_second)
    coefficients = jnp.fft.rfftn(volume, axes=(0, 1, 3))
    index_x = kept_modes(MX, X)
    index_y = kept_modes(MY, Y)
    picked = coefficients[index_x][:, index_y][:, :, :, :MZ]
    part_real = jnp.real(picked)
    part_imag = jnp.imag(picked)
    weight_real = spec_real.reshape(2 * MX, 2 * MY, C, MZ, C)
    weight_imag = spec_imag.reshape(2 * MX, 2 * MY, C, MZ, C)
    mixed_real = jnp.einsum("abik,abiko->abok", part_real, weight_real, precision=highest) - jnp.einsum("abik,abiko->abok", part_imag, weight_imag, precision=highest)
    mixed_imag = jnp.einsum("abik,abiko->abok", part_real, weight_imag, precision=highest) + jnp.einsum("abik,abiko->abok", part_imag, weight_real, precision=highest)
    full_real = jnp.zeros((X, Y, C, Z // 2 + 1), jnp.float32).at[index_x[:, None], index_y[None, :], :, :MZ].set(mixed_real)
    full_imag = jnp.zeros((X, Y, C, Z // 2 + 1), jnp.float32).at[index_x[:, None], index_y[None, :], :, :MZ].set(mixed_imag)
    spectral = jnp.fft.irfftn(full_real + 1j * full_imag, s=(X, Y, Z), axes=(0, 1, 3))
    layer_out = jax.nn.gelu(spectral + conv_out, approximate=False)
    return layer_out.reshape(X, Y, C * Z)
```

```python
import jax
import jax.numpy as jnp
import numpy as np
from jax import lax
from jax.experimental import pallas as pl
from jax.experimental.pallas import tpu as pltpu
from jax.sharding import PartitionSpec as P

C = 36
Z = 64
MZ = 12
X = 128
Y = 128
GX = 32
GY = 16
NX = 4
NY = 8
GROUP = 8
KB = 112
F32 = jnp.float32
BF16 = jnp.bfloat16
MESH = pl.DeviceIdType.MESH


def halves(table):
    high = table.astype(jnp.bfloat16)
    low = (table - high.astype(np.float64)).astype(jnp.bfloat16)
    return high, low


def stacked(table, pad=0):
    high, low = halves(table)
    parts = [high, high, low]
    if pad:
        parts.append(np.zeros(high.shape[:-1] + (pad,), high.dtype))
    return np.concatenate(parts, axis=-1)


def tables():
    r = np.arange(MZ)
    z = np.arange(Z)
    zr = 2 * np.pi * np.outer(z, r) / Z
    forward = np.zeros((704, 256))
    backward = np.zeros((2, 256, 640))
    weight = np.where(r == 0, 1.0, 2.0) / (X * Y * Z)
    for c in range(9):
        rows = slice(64 + c * Z, 64 + c * Z + Z)
        forward[rows, c * MZ : c * MZ + MZ] = np.cos(zr)
        forward[rows, 128 + c * MZ : 128 + c * MZ + MZ] = -np.sin(zr)
        for e in range(2):
            cols = slice(64 * e + c * Z, 64 * e + c * Z + Z)
            backward[e, c * MZ : c * MZ + MZ, cols] = (np.cos(zr) * weight).T
            backward[e, 128 + c * MZ : 128 + c * MZ + MZ, cols] = -(np.sin(zr) * weight).T
    freq = np.where(np.arange(32) < 16, np.arange(32), np.arange(32) + 96)

    def pair(first, second):
        angle = 2 * np.pi * (np.outer(first, second) % 128) / 128
        return np.concatenate([np.cos(angle), np.sin(angle)], axis=0)

    xs = [np.arange(32) + 32 * g for g in range(4)]
    ys = [np.arange(NY) + NY * g for g in range(GY)]
    d1 = stacked(np.stack([pair(freq, v) for v in xs]))
    d2 = stacked(np.stack([pair(freq, v) for v in ys]), 8)
    d4 = stacked(np.stack([pair(v, freq) for v in ys]))
    d5 = stacked(np.stack([pair(v, freq) for v in xs]))
    mask = np.zeros((4, 40, 128), np.float32)
    spread = np.zeros((128, 512))
    order = np.zeros((512, 512))
    for c in range(C):
        mask[c // 9, c, (c % 9) * MZ : (c % 9) * MZ + MZ] = 1
    for c in range(9):
        for k in range(MZ):
            spread[c * MZ + k, k * C : k * C + C] = 1
    for k in range(MZ):
        for o in range(C):
            order[k * C + o, (o // 9) * 128 + (o % 9) * MZ + k] = 1
    return (
        np.stack(halves(forward)),
        d1,
        d2,
        d4,
        d5,
        mask,
        spread.astype(jnp.bfloat16),
        order.astype(jnp.bfloat16),
        np.stack(halves(backward), axis=1),
    )


def split(value):
    high = value.astype(BF16)
    low = (value - high.astype(F32)).astype(BF16)
    return high, low


def split32(value):
    high = value.astype(BF16).astype(F32)
    return high, value - high


def dot(left, right):
    return jnp.dot(left, right, preferred_element_type=F32)


def gelu(value):
    return 0.5 * value * (1.0 + lax.erf(value * 0.7071067811865476))


def kernel(
    state_hbm, wf_hbm, ws_hbm, sr_hbm, si_hbm,
    fz_hbm, d1_hbm, d2_hbm, d4_hbm, d5_hbm, mk_hbm, ex_hbm, pm_hbm, fi_hbm,
    out_ref,
    st, wf, ws, sr, si, fz, d1, d2, d4, d5, mk, ex, pm, fi,
    s1, r1, s2, r2, s3, r3, s4, r4, s5, r5, s6, r6,
    tt, m8, wst1, wst2, cc, stage, ubh, ubl, hid, stage2, ub2h, ub2l, ct, n2, co,
    load_sem, send_sem, recv_sem, halo_send, halo_recv,
):
    i = lax.axis_index("gx")
    j = lax.axis_index("gy")
    a = i // GROUP
    l = i % GROUP

    sources = [
        (state_hbm, st), (fz_hbm, fz), (d1_hbm.at[a], d1), (d2_hbm.at[j], d2), (wf_hbm, wf),
        (ws_hbm, ws), (sr_hbm.at[0], sr), (si_hbm.at[0], si), (mk_hbm, mk), (ex_hbm, ex),
        (pm_hbm, pm), (d4_hbm.at[j], d4), (d5_hbm.at[a], d5), (fi_hbm, fi),
    ]
    loads = [pltpu.make_async_copy(src, dst, load_sem.at[n]) for n, (src, dst) in enumerate(sources)]
    for load in loads:
        load.start()
    (l_st, l_fz, l_d1, l_d2, l_wf, l_ws, l_sr, l_si, l_mk, l_ex, l_pm, l_d4, l_d5, l_fi) = loads

    barrier = pltpu.get_barrier_semaphore()

    @pl.loop(1, GX)
    def _(s):
        pl.semaphore_signal(barrier, inc=1, device_id=((i + s) % GX, j), device_id_type=MESH)

    @pl.loop(1, GY)
    def _(s):
        pl.semaphore_signal(barrier, inc=1, device_id=(i, (j + s) % GY), device_id_type=MESH)

    def remote(src, dst, stage_no, device):
        return pltpu.make_async_remote_copy(
            src_ref=src, dst_ref=dst, send_sem=send_sem.at[stage_no], recv_sem=recv_sem.at[stage_no],
            device_id=device, device_id_type=MESH,
        )

    def rows(start, size):
        return pl.ds(pl.multiple_of(start, 8), size)

    def wait_recv(buffer, count, stage_no):
        part = buffer.at[pl.ds(0, count)]
        pltpu.make_async_copy(part, part, recv_sem.at[stage_no]).wait()

    def wait_send(buffer, count, stage_no):
        part = buffer.at[pl.ds(0, count)]
        pltpu.make_async_copy(part, part, send_sem.at[stage_no]).wait()

    lane = lax.broadcasted_iota(jnp.int32, (1, 128), 1)
    first_half = lane < 64

    cc[...] = jnp.zeros_like(cc)
    l_st.wait()
    t2 = tt.reshape(8 * 12 * 24, 128)
    for x in range(NX):
        for m in range(18):
            t2[pl.ds(((x + 2) * 12 + 2) * 24 + m, 8, stride=24), :] = st[x, :, m * 128 : (m + 1) * 128]
    l_fz.wait()
    field = st[...].reshape(NX * NY, C * Z)
    for e in range(2):
        left = jnp.concatenate([field[:, h * 1152 + e * 512 : h * 1152 + e * 512 + 640] for h in range(2)], axis=0)
        high, low = split(left)
        fh = fz[0, 64 * (1 - e) : 64 * (1 - e) + 640, :]
        fl = fz[1, 64 * (1 - e) : 64 * (1 - e) + 640, :]
        res = dot(high, fh) + dot(low, fh) + dot(high, fl)
        for h in range(2):
            for part in range(2):
                for x in range(NX):
                    s1[pl.ds(x * 8 + part * 4 + 2 * h + e, 8, stride=32), :] = res[
                        h * 32 + x * 8 : h * 32 + x * 8 + 8, part * 128 : part * 128 + 128
                    ]
    pl.semaphore_wait(barrier, GX - 1 + GY - 1)

    @pl.loop(1, GROUP)
    def _(s):
        t = (l + s) % GROUP
        remote(s1.at[rows(t * 32, 32)], r1.at[rows(l * 32, 32)], 0, (a * GROUP + t, j)).start()

    r1[rows(l * 32, 32), :] = s1[rows(l * 32, 32), :]

    def halo(n, src, dst, device):
        return pltpu.make_async_remote_copy(
            src_ref=src, dst_ref=dst, send_sem=halo_send.at[n], recv_sem=halo_recv.at[n],
            device_id=device, device_id_type=MESH,
        )

    down_y = halo(0, tt.at[2:6, 2:4], tt.at[2:6, 10:12], (i, (j + GY - 1) % GY))
    up_y = halo(1, tt.at[2:6, 8:10], tt.at[2:6, 0:2], (i, (j + 1) % GY))
    down_x = halo(2, tt.at[2:4], tt.at[6:8], ((i + GX - 1) % GX, j))
    up_x = halo(3, tt.at[4:6], tt.at[0:2], ((i + 1) % GX, j))

    @pl.when(j > 0)
    def _():
        down_y.start()

    @pl.when(j < GY - 1)
    def _():
        up_y.start()

    @pl.when(j == 0)
    def _():
        tt[2:6, 0:2] = jnp.zeros((4, 2, 24, 128), F32)

    @pl.when(j == GY - 1)
    def _():
        tt[2:6, 10:12] = jnp.zeros((4, 2, 24, 128), F32)

    @pl.when(i == 0)
    def _():
        tt[0:2] = jnp.zeros((2, 12, 24, 128), F32)

    @pl.when(i == GX - 1)
    def _():
        tt[6:8] = jnp.zeros((2, 12, 24, 128), F32)

    def filters(src, scratch):
        scratch[...] = jnp.zeros_like(scratch)
        for tap_x in range(3):
            for tap_y in range(3):
                tap = tap_x * 3 + tap_y
                high, low = split32(src[tap_x, tap_y])
                scratch[0:36, tap * KB : tap * KB + 108] = high
                scratch[40:76, tap * KB : tap * KB + 108] = low

    l_wf.wait()
    filters(wf, wst1)

    wait_recv(r1, 7 * 32, 0)
    l_d1.wait()

    def gathered(buffer):
        return jnp.concatenate([buffer[pl.ds(k, 32, stride=8), :] for k in range(8)], axis=1)

    def tripled(value):
        high, low = split(value)
        return jnp.concatenate([high, low, high], axis=0)

    def combine(res, count, sign):
        top, bottom = res[:count], res[count:]
        real = top[:, :512] + sign * bottom[:, 512:]
        imag = top[:, 512:] - sign * bottom[:, :512]
        return real, imag

    def scatter_rows(buffer, real, imag, count):
        for k in range(4):
            buffer[pl.ds(k, count, stride=8), :] = real[:, k * 128 : k * 128 + 128]
            buffer[pl.ds(k + 4, count, stride=8), :] = imag[:, k * 128 : k * 128 + 128]

    res = dot(d1[...], tripled(gathered(r1)))
    real, imag = combine(res, 32, 1.0)
    scatter_rows(s2, real, imag, 32)

    @pl.loop(1, GX)
    def _(s):
        t = (i + s) % GX
        remote(s2.at[rows(t * 8, 8)], r2.at[rows(i * 8, 8)], 1, (t, j)).start()

    r2[rows(i * 8, 8), :] = s2[rows(i * 8, 8), :]
    l_ws.wait()
    filters(ws, wst2)

    wait_recv(r2, 31 * 8, 1)
    l_d2.wait()
    summed = []
    for k in range(8):
        total = r2[pl.ds(k, 8, stride=8), :]
        for g in range(1, 4):
            total = total + r2[pl.ds(g * 64 + k, 8, stride=8), :]
        summed.append(total)
    high, low = split32(jnp.concatenate(summed, axis=1))
    right = jnp.concatenate([high, low, high, jnp.zeros_like(high)], axis=0).astype(BF16)
    real, imag = combine(dot(d2[...], right), 32, 1.0)
    scatter_rows(s3, real, imag, 32)

    @pl.loop(1, GY)
    def _(s):
        t = (j + s) % GY
        remote(s3.at[rows(t * 16, 16)], r3.at[rows(j * 16, 16)], 2, (i, t)).start()

    r3[rows(j * 16, 16), :] = s3[rows(j * 16, 16), :]

    @pl.when(j > 0)
    def _():
        up_y.wait_recv()

    @pl.when(j < GY - 1)
    def _():
        down_y.wait_recv()

    @pl.when(i > 0)
    def _():
        down_x.start()

    @pl.when(i < GX - 1)
    def _():
        up_x.start()

    wait_recv(r3, 15 * 16, 2)
    total = r3[0:16, :]
    for n in range(1, GY):
        total = total + r3[n * 16 : n * 16 + 16, :]
    for load in (l_mk, l_ex, l_sr, l_si, l_pm):
        load.wait()
    placed = []
    for q in range(2):
        for part in range(2):
            acc = None
            for g in range(4):
                n = q * 8 + part * 4 + g
                term = total[n : n + 1, :] * mk[g]
                acc = term if acc is None else acc + term
            placed.append(acc)
    high, low = split(jnp.concatenate(placed, axis=0))
    wide = dot(high, ex[...]) + dot(low, ex[...])
    m8[...] = jnp.zeros_like(m8)
    for q in range(2):
        c_re = wide[q * 80 : q * 80 + 36, :432]
        c_im = wide[q * 80 + 40 : q * 80 + 76, :432]
        m8[2 * q : 2 * q + 1, 0:432] = jnp.sum(c_re * sr[q] - c_im * si[q], axis=0, keepdims=True)
        m8[2 * q + 1 : 2 * q + 2, 0:432] = jnp.sum(c_re * si[q] + c_im * sr[q], axis=0, keepdims=True)
    high, low = split32(m8[...])
    moved = dot(jnp.concatenate([high, low], axis=0).astype(BF16), pm[...])
    mixed = moved[0:8] + moved[8:16]
    for g in range(4):
        s4[pl.ds(g, 4, stride=4), :] = mixed[0:4, g * 128 : g * 128 + 128]

    @pl.loop(1, GY)
    def _(s):
        t = (j + s) % GY
        remote(s4, r4.at[rows(j * 16, 16)], 3, (i, t)).start()

    r4[rows(j * 16, 16), :] = s4[...]

    @pl.when(i > 0)
    def _():
        up_x.wait_recv()

    @pl.when(i < GX - 1)
    def _():
        down_x.wait_recv()

    z_of = lane % 64

    def shifted(value, d):
        if d == 0:
            return jnp.where(z_of == 0, 0.0, pltpu.roll(value, 1, axis=1))
        if d == 2:
            return jnp.where(z_of == 63, 0.0, pltpu.roll(value, 127, axis=1))
        return value

    def columns(value, buffer, base):
        for d in range(3):
            buffer[base + d * 36 : base + d * 36 + 36, :] = shifted(value, d)[0:36]
        return split(buffer[base : base + KB, :])

    stage[...] = jnp.zeros_like(stage)
    stage2[...] = jnp.zeros_like(stage2)

    @pl.loop(0, 8)
    def _(x):
        for u in range(7):
            near = t2[rows((x * 12 + u) * 24, 24), :]
            far = t2[rows((x * 12 + u + 5) * 24, 24), :]
            even = jnp.where(first_half, near, pltpu.roll(far, 64, axis=1))
            odd = jnp.where(first_half, pltpu.roll(near, 64, axis=1), far)
            cc[pl.ds(u * 40, 18, stride=2), :] = even[0:18]
            cc[pl.ds(u * 40 + 1, 18, stride=2), :] = odd[0:18]
            high, low = columns(cc[u * 40 : u * 40 + 40, :], stage, u * KB)
            for b in range(3):
                v = u - b
                if 0 <= v < 5:
                    place = pl.ds(pl.multiple_of(x * 336 + b * KB, 16), KB)
                    ubh[place, v * 128 : v * 128 + 128] = high
                    ubl[place, v * 128 : v * 128 + 128] = low

    w1 = wst1[...].astype(BF16)
    wide_lane = lax.broadcasted_iota(jnp.int32, (1, 640), 1)
    keep_y = jnp.where((wide_lane < 64) & (j == 0), 0.0, 1.0) * jnp.where(
        (wide_lane >= 576) & (j == GY - 1), 0.0, 1.0
    )

    @pl.loop(0, 6)
    def _(x):
        place = pl.ds(pl.multiple_of(x * 336, 16), 1008)
        res = dot(w1, ubh[place, :])
        value = res[0:40] + res[40:80] + dot(w1[0:40], ubl[place, :])
        outside = ((x == 0) & (i == 0)) | ((x == 5) & (i == GX - 1))
        keep = keep_y * jnp.where(outside, 0.0, 1.0)
        hid[rows(x * 40, 40), :] = gelu(value) * keep

    wait_recv(r4, 15 * 16, 3)
    l_d4.wait()
    real, imag = combine(dot(d4[...], tripled(gathered(r4))), 8, -1.0)
    scatter_rows(s5, real, imag, 8)

    @pl.loop(1, GX)
    def _(s):
        t = (i + s) % GX
        remote(s5.at[rows((t % GROUP) * 8, 8)], r5.at[rows(i * 8, 8)], 4, (t, j)).start()

    r5[rows(i * 8, 8), :] = s5[rows(l * 8, 8), :]

    @pl.loop(0, 6)
    def _(x):
        pairs = [hid[rows(x * 40, 40), v * 128 : v * 128 + 128] for v in range(5)]
        units = [(pairs[n], [(b, n - b) for b in range(3) if 0 <= n - b < 3]) for n in range(5)]
        units.append((jnp.where(first_half, pairs[3], pltpu.roll(pairs[4], 64, axis=1)), [(0, 3)]))
        units.append((jnp.where(first_half, pairs[4], pairs[0]), [(1, 3)]))
        units.append((jnp.where(first_half, pltpu.roll(pairs[0], 64, axis=1), pairs[1]), [(2, 3)]))
        for n, (value, places) in enumerate(units):
            high, low = columns(value, stage2, n * KB)
            for b, v in places:
                place = pl.ds(pl.multiple_of(x * 336 + b * KB, 16), KB)
                ub2h[place, v * 128 : v * 128 + 128] = high
                ub2l[place, v * 128 : v * 128 + 128] = low

    wait_recv(r5, 31 * 8, 4)
    l_d5.wait()
    real, imag = combine(dot(d5[...], tripled(gathered(r5))), 32, -1.0)
    scatter_rows(s6, real, imag, 32)

    @pl.loop(1, GROUP)
    def _(s):
        t = (l + s) % GROUP
        remote(s6.at[rows(t * 32, 32)], r6.at[rows(l * 32, 32)], 5, (a * GROUP + t, j)).start()

    r6[rows(l * 32, 32), :] = s6[rows(l * 32, 32), :]

    w2 = wst2[...].astype(BF16)

    @pl.loop(0, NX)
    def _(x):
        place = pl.ds(pl.multiple_of(x * 336, 16), 1008)
        res = dot(w2, ub2h[place, :])
        value = res[0:40] + res[40:80] + dot(w2[0:40], ub2l[place, :])
        for v in range(4):
            ct[v * 40 : v * 40 + 40, :] = value[:, v * 128 : v * 128 + 128]
        for v in range(4):
            even = ct[pl.ds(v * 40, 18, stride=2), :]
            odd = ct[pl.ds(v * 40 + 1, 18, stride=2), :]
            near = jnp.where(first_half, even, pltpu.roll(odd, 64, axis=1))
            far = jnp.where(first_half, pltpu.roll(even, 64, axis=1), odd)
            y_near, y_far = (v, v + 5) if v < 3 else (3, 4)
            n2[y_near * 24 : y_near * 24 + 18, :] = near
            n2[y_far * 24 : y_far * 24 + 18, :] = far
        for m in range(18):
            co[rows(x * 8, 8), m * 128 : m * 128 + 128] = n2[pl.ds(m, 8, stride=24), :]

    wait_recv(r6, 7 * 32, 5)
    l_fi.wait()
    results = []
    for e in range(2):
        left = jnp.concatenate(
            [
                jnp.concatenate(
                    [
                        jnp.concatenate(
                            [r6[pl.ds(x * 8 + part * 4 + 2 * h + e, 8, stride=32), :] for x in range(NX)], axis=0
                        )
                        for part in range(2)
                    ],
                    axis=1,
                )
                for h in range(2)
            ],
            axis=0,
        )
        high, low = split(left)
        results.append(dot(high, fi[e, 0]) + dot(low, fi[e, 0]) + dot(high, fi[e, 1]))
    for h in range(2):
        one, two = results[0][h * 32 : h * 32 + 32], results[1][h * 32 : h * 32 + 32]
        spectral = jnp.concatenate([one[:, :512], one[:, 512:] + two[:, :128], two[:, 128:]], axis=1)
        full = spectral + co[:, h * 1152 : h * 1152 + 1152]
        for x in range(NX):
            out_ref[x, :, h * 1152 : h * 1152 + 1152] = full[x * 8 : x * 8 + 8]

    wait_send(s1, 7 * 32, 0)
    wait_send(s2, 31 * 8, 1)
    wait_send(s3, 15 * 16, 2)
    wait_send(r4, 15 * 16, 3)
    wait_send(r5, 31 * 8, 4)
    wait_send(s6, 7 * 32, 5)

    @pl.when(j > 0)
    def _():
        down_y.wait_send()

    @pl.when(j < GY - 1)
    def _():
        up_y.wait_send()

    @pl.when(i > 0)
    def _():
        down_x.wait_send()

    @pl.when(i < GX - 1)
    def _():
        up_x.wait_send()


def on_device(state_field, conv_first, conv_second, spec_real, spec_imag):
    constants = [jnp.asarray(t) for t in tables()]
    vm = pltpu.VMEM
    scratch = [
        vm((NX, NY, C * Z), F32), vm((3, 3, C, 3 * C), F32), vm((3, 3, C, 3 * C), F32),
        vm((2, C, MZ * C), F32), vm((2, C, MZ * C), F32),
        vm((2, 704, 256), BF16), vm((64, 96), BF16), vm((64, 32), BF16), vm((16, 96), BF16), vm((64, 96), BF16),
        vm((4, 40, 128), F32), vm((128, 512), BF16), vm((512, 512), BF16), vm((2, 2, 256, 640), BF16),
        vm((256, 128), F32), vm((256, 128), F32), vm((256, 128), F32), vm((256, 128), F32),
        vm((256, 128), F32), vm((256, 128), F32), vm((16, 128), F32), vm((256, 128), F32),
        vm((64, 128), F32), vm((256, 128), F32), vm((256, 128), F32), vm((256, 128), F32),
        vm((8, 12, 24, 128), F32), vm((8, 512), F32), vm((80, 9 * KB), F32), vm((80, 9 * KB), F32),
        vm((280, 128), F32), vm((7 * KB, 128), F32), vm((8 * 336, 640), BF16), vm((8 * 336, 640), BF16),
        vm((240, 640), F32), vm((8 * KB, 128), F32), vm((6 * 336, 512), BF16), vm((6 * 336, 512), BF16),
        vm((160, 128), F32), vm((192, 128), F32), vm((32, C * Z), F32),
        pltpu.SemaphoreType.DMA((14,)), pltpu.SemaphoreType.DMA((6,)), pltpu.SemaphoreType.DMA((6,)),
        pltpu.SemaphoreType.DMA((4,)), pltpu.SemaphoreType.DMA((4,)),
    ]
    before = pl.pallas_call(
        kernel,
        out_shape=jax.ShapeDtypeStruct((NX, NY, C * Z), F32),
        in_specs=[pl.BlockSpec(memory_space=pl.ANY)] * (5 + len(constants)),
        out_specs=pl.BlockSpec(memory_space=pltpu.VMEM),
        scratch_shapes=scratch,
        compiler_params=pltpu.CompilerParams(
            collective_id=0, has_side_effects=True, vmem_limit_bytes=40 * 1024 * 1024
        ),
    )(state_field, conv_first, conv_second, spec_real, spec_imag, *constants)
    return jax.nn.gelu(before, approximate=False)


def solution(mesh):
    in_specs = (P("gx", "gy", None), P(), P(), P("gx", "gy", None, None), P("gx", "gy", None, None))
    return jax.shard_map(
        on_device, mesh=mesh, in_specs=in_specs, out_specs=P("gx", "gy", None), check_vma=False
    )
```

```python
import jax
import jax.numpy as jnp
import numpy as np
from jax import lax
from jax.experimental import pallas as pl
from jax.experimental.pallas import tpu as pltpu
from jax.sharding import PartitionSpec as P

C = 36
Z = 64
MZ = 12
X = 128
Y = 128
GX = 32
GY = 16
NX = 4
NY = 8
GROUP = 8
KB = 112
F32 = jnp.float32
BF16 = jnp.bfloat16
MESH = pl.DeviceIdType.MESH


def halves(table):
    high = table.astype(jnp.bfloat16)
    low = (table - high.astype(np.float64)).astype(jnp.bfloat16)
    return high, low


def stacked(table):
    high, low = halves(table)
    return np.concatenate([high, high, low], axis=-1)


def tables():
    r = np.arange(MZ)
    z = np.arange(Z)
    zr = 2 * np.pi * np.outer(z, r) / Z
    forward = np.zeros((704, 256))
    backward = np.zeros((2, 256, 640))
    weight = np.where(r == 0, 1.0, 2.0) / (X * Y * Z)
    for c in range(9):
        rows = slice(64 + c * Z, 64 + c * Z + Z)
        forward[rows, c * MZ : c * MZ + MZ] = np.cos(zr)
        forward[rows, 128 + c * MZ : 128 + c * MZ + MZ] = -np.sin(zr)
        for e in range(2):
            cols = slice(64 * e + c * Z, 64 * e + c * Z + Z)
            backward[e, c * MZ : c * MZ + MZ, cols] = (np.cos(zr) * weight).T
            backward[e, 128 + c * MZ : 128 + c * MZ + MZ, cols] = -(np.sin(zr) * weight).T
    freq = np.where(np.arange(32) < 16, np.arange(32), np.arange(32) + 96)

    def pair(first, second):
        angle = 2 * np.pi * (np.outer(first, second) % 128) / 128
        return np.concatenate([np.cos(angle), np.sin(angle)], axis=0)

    members = np.array([[(t // 2) * 8 + g * 2 + t % 2 for t in range(GROUP)] for g in range(4)])
    xs = [(members[g][:, None] * NX + np.arange(NX)[None, :]).reshape(32) for g in range(4)]
    blocks = np.arange(4) * 4
    ys = [((blocks[:, None] + g) * NY + np.arange(NY)[None, :]).reshape(32) for g in range(4)]
    halved = np.concatenate([freq[0::2], freq[1::2]])
    d1 = stacked(np.stack([pair(freq, v) for v in xs]))
    d2 = stacked(np.stack([pair(halved, v) for v in ys]))
    d4 = stacked(np.stack([pair(v, halved) for v in ys]))
    d5 = stacked(np.stack([pair(v, freq) for v in xs]))
    mask = np.zeros((4, 40, 128), np.float32)
    spread = np.zeros((128, 512))
    order = np.zeros((512, 512))
    for c in range(C):
        mask[c // 9, c, (c % 9) * MZ : (c % 9) * MZ + MZ] = 1
    for c in range(9):
        for k in range(MZ):
            spread[c * MZ + k, k * C : k * C + C] = 1
    for k in range(MZ):
        for o in range(C):
            order[k * C + o, (o // 9) * 128 + (o % 9) * MZ + k] = 1
    return (
        np.stack(halves(forward)),
        d1,
        d2,
        d4,
        d5,
        mask,
        spread.astype(jnp.bfloat16),
        order.astype(jnp.bfloat16),
        np.stack(halves(backward), axis=1),
    )


def split(value):
    high = value.astype(BF16)
    low = (value - high.astype(F32)).astype(BF16)
    return high, low


def split32(value):
    high = value.astype(BF16).astype(F32)
    return high, value - high


def dot(left, right):
    return jnp.dot(left, right, preferred_element_type=F32)


def gelu(value):
    return 0.5 * value * (1.0 + lax.erf(value * 0.7071067811865476))


def kernel(
    state_hbm, wf_hbm, ws_hbm, sr_hbm, si_hbm,
    fz_hbm, d1_hbm, d2_hbm, d4_hbm, d5_hbm, mk_hbm, ex_hbm, pm_hbm, fi_hbm,
    out_ref,
    st, wf, ws, sr, si, fz, d1, d2, d4, d5, mk, ex, pm, fi,
    s1, r1, s2, r2, s3, r3, s4, r4, s5, r5, s6, r6,
    tt, m8, wst1, wst2, cc, stage, ubh, ubl, hid, stage2, ub2h, ub2l, ct, n2, co,
    load_sem, send_sem, recv_sem, halo_send, halo_recv,
):
    i = lax.axis_index("gx")
    j = lax.axis_index("gy")
    g = (i % 8) // 2
    l = (i // 8) * 2 + i % 2
    yy = j // 4
    zz = j % 4

    sources = [
        (state_hbm, st), (fz_hbm, fz), (d1_hbm.at[g], d1), (d2_hbm.at[zz], d2), (wf_hbm, wf),
        (ws_hbm, ws), (sr_hbm, sr), (si_hbm, si), (mk_hbm, mk), (ex_hbm, ex),
        (pm_hbm, pm), (d4_hbm.at[zz], d4), (d5_hbm.at[g], d5), (fi_hbm, fi),
    ]
    loads = [pltpu.make_async_copy(src, dst, load_sem.at[n]) for n, (src, dst) in enumerate(sources)]
    loads[0].start()
    loads[1].start()
    (l_st, l_fz, l_d1, l_d2, l_wf, l_ws, l_sr, l_si, l_mk, l_ex, l_pm, l_d4, l_d5, l_fi) = loads

    def peer(t, y):
        return ((t // 2) * 8 + g * 2 + t % 2, y * 4 + zz)

    barrier = pltpu.get_barrier_semaphore()

    @pl.loop(1, GX)
    def _(s):
        pl.semaphore_signal(barrier, inc=1, device_id=((i + s) % GX, j), device_id_type=MESH)

    @pl.loop(1, GY)
    def _(s):
        pl.semaphore_signal(barrier, inc=1, device_id=(i, (j + s) % GY), device_id_type=MESH)

    @pl.loop(1, GROUP)
    def _(s):
        for n in range(1, 4):
            pl.semaphore_signal(
                barrier, inc=1, device_id=peer((l + s) % GROUP, (yy + n) % 4), device_id_type=MESH
            )


    def remote(src, dst, stage_no, device):
        return pltpu.make_async_remote_copy(
            src_ref=src, dst_ref=dst, send_sem=send_sem.at[stage_no], recv_sem=recv_sem.at[stage_no],
            device_id=device, device_id_type=MESH,
        )

    def rows(start, size):
        return pl.ds(pl.multiple_of(start, 8), size)

    def wait_recv(buffer, count, stage_no):
        part = buffer.at[pl.ds(0, count)]
        pltpu.make_async_copy(part, part, recv_sem.at[stage_no]).wait()

    def wait_send(buffer, count, stage_no):
        part = buffer.at[pl.ds(0, count)]
        pltpu.make_async_copy(part, part, send_sem.at[stage_no]).wait()

    lane = lax.broadcasted_iota(jnp.int32, (1, 128), 1)
    first_half = lane < 64

    l_st.wait()
    l_fz.wait()
    field = st[...].reshape(NX * NY, C * Z)
    for e in range(2):
        left = jnp.concatenate([field[:, h * 1152 + e * 512 : h * 1152 + e * 512 + 640] for h in range(2)], axis=0)
        high, low = split(left)
        fh = fz[0, 64 * (1 - e) : 64 * (1 - e) + 640, :]
        fl = fz[1, 64 * (1 - e) : 64 * (1 - e) + 640, :]
        res = dot(high, fh) + dot(low, fh) + dot(high, fl)
        for h in range(2):
            for part in range(2):
                for x in range(NX):
                    s1[pl.ds((2 * h + e) * 64 + x * 2 + part, 8, stride=8), :] = res[
                        h * 32 + x * 8 : h * 32 + x * 8 + 8, part * 128 : part * 128 + 128
                    ]
    pl.semaphore_wait(barrier, GX - 1 + GY - 1 + 21)
    slot = yy * 8 + l

    @pl.loop(1, 32)
    def _(s):
        n = (slot + s) % 32
        remote(s1.at[rows(n * 8, 8)], r1.at[rows(slot * 8, 8)], 0, peer(n % 8, n // 8)).start()

    r1[rows(slot * 8, 8), :] = s1[rows(slot * 8, 8), :]
    for load in loads[2:]:
        load.start()

    cc[...] = jnp.zeros_like(cc)
    t2 = tt.reshape(8 * 12 * 24, 128)
    for x in range(NX):
        for m in range(18):
            t2[pl.ds(((x + 2) * 12 + 2) * 24 + m, 8, stride=24), :] = st[x, :, m * 128 : (m + 1) * 128]

    def halo(n, src, dst, device):
        return pltpu.make_async_remote_copy(
            src_ref=src, dst_ref=dst, send_sem=halo_send.at[n], recv_sem=halo_recv.at[n],
            device_id=device, device_id_type=MESH,
        )

    down_y = halo(0, tt.at[2:6, 2:4], tt.at[2:6, 10:12], (i, (j + GY - 1) % GY))
    up_y = halo(1, tt.at[2:6, 8:10], tt.at[2:6, 0:2], (i, (j + 1) % GY))
    down_x = halo(2, tt.at[2:4], tt.at[6:8], ((i + GX - 1) % GX, j))
    up_x = halo(3, tt.at[4:6], tt.at[0:2], ((i + 1) % GX, j))

    @pl.when(j == 0)
    def _():
        tt[2:6, 0:2] = jnp.zeros((4, 2, 24, 128), F32)

    @pl.when(j == GY - 1)
    def _():
        tt[2:6, 10:12] = jnp.zeros((4, 2, 24, 128), F32)

    @pl.when(i == 0)
    def _():
        tt[0:2] = jnp.zeros((2, 12, 24, 128), F32)

    @pl.when(i == GX - 1)
    def _():
        tt[6:8] = jnp.zeros((2, 12, 24, 128), F32)

    def filters(src, scratch):
        scratch[...] = jnp.zeros_like(scratch)
        for tap_x in range(3):
            for tap_y in range(3):
                tap = tap_x * 3 + tap_y
                high, low = split32(src[tap_x, tap_y])
                scratch[0:36, tap * KB : tap * KB + 108] = high
                scratch[40:76, tap * KB : tap * KB + 108] = low

    @pl.when(j > 0)
    def _():
        down_y.start()

    @pl.when(j < GY - 1)
    def _():
        up_y.start()

    l_wf.wait()
    filters(wf, wst1)

    wait_recv(r1, 31 * 8, 0)
    l_d1.wait()

    def gathered(buffer):
        return jnp.concatenate([buffer[pl.ds(k, 32, stride=8), :] for k in range(8)], axis=1)

    def tripled(value):
        high, low = split(value)
        return jnp.concatenate([high, low, high], axis=0)

    def exchanged(buffer):
        return jnp.concatenate(
            [buffer[pl.ds(y * 64 + part, 32, stride=2), :] for part in range(2) for y in range(4)], axis=1
        )

    def combine(res, sign):
        half = res.shape[1] // 2
        top, bottom = res[:32], res[32:]
        real = top[:, :half] + sign * bottom[:, half:]
        imag = top[:, half:] - sign * bottom[:, :half]
        return real, imag

    real, imag = combine(dot(d1[...], tripled(exchanged(r1))), 1.0)
    for k in range(4):
        s2[pl.ds(k, 32, stride=8), :] = real[:, k * 128 : k * 128 + 128]
        s2[pl.ds(k + 4, 32, stride=8), :] = imag[:, k * 128 : k * 128 + 128]

    @pl.loop(1, GX)
    def _(s):
        t = (i + s) % GX
        remote(s2.at[rows(t * 8, 8)], r2.at[rows((g * 8 + l) * 8, 8)], 1, (t, j)).start()

    r2[rows((g * 8 + l) * 8, 8), :] = s2[rows(i * 8, 8), :]
    l_ws.wait()
    filters(ws, wst2)

    wait_recv(r2, 31 * 8, 1)
    l_d2.wait()
    parts = []
    for part in range(2):
        column = []
        for y in range(4):
            k = part * 4 + y
            terms = [r2[pl.ds(n * 64 + k, 8, stride=8), :] for n in range(4)]
            column.append((terms[0] + terms[1]) + (terms[2] + terms[3]))
        parts.append(jnp.concatenate(column, axis=0))
    result = combine(dot(d2[...], tripled(jnp.concatenate(parts, axis=1))), 1.0)
    for b in range(2):
        for part in range(2):
            s3[:, b * 2 + part, :] = result[part][b * 16 : b * 16 + 16]

    @pl.loop(1, GY)
    def _(s):
        t = (j + s) % GY
        remote(s3.at[t], r3.at[j], 2, (i, t)).start()

    r3[j] = s3[j]

    @pl.when(j > 0)
    def _():
        up_y.wait_recv()

    @pl.when(j < GY - 1)
    def _():
        down_y.wait_recv()

    @pl.when(i > 0)
    def _():
        down_x.start()

    @pl.when(i < GX - 1)
    def _():
        up_x.start()

    wait_recv(r3, GY - 1, 2)
    total = [(r3[4 * n] + r3[4 * n + 1]) + (r3[4 * n + 2] + r3[4 * n + 3]) for n in range(4)]
    for load in (l_mk, l_ex, l_sr, l_si, l_pm):
        load.wait()
    placed = []
    for q in range(2):
        for part in range(2):
            acc = None
            for cg in range(4):
                n = q * 2 + part
                term = total[cg][n : n + 1, :] * mk[cg]
                acc = term if acc is None else acc + term
            placed.append(acc)
    high, low = split(jnp.concatenate(placed, axis=0))
    wide = dot(high, ex[...]) + dot(low, ex[...])
    m8[...] = jnp.zeros_like(m8)
    for q in range(2):
        c_re = wide[q * 80 : q * 80 + 36, :432]
        c_im = wide[q * 80 + 40 : q * 80 + 76, :432]
        w_re, w_im = sr[:, q, :], si[:, q, :]
        m8[2 * q : 2 * q + 1, 0:432] = jnp.sum(c_re * w_re - c_im * w_im, axis=0, keepdims=True)
        m8[2 * q + 1 : 2 * q + 2, 0:432] = jnp.sum(c_re * w_im + c_im * w_re, axis=0, keepdims=True)
    high, low = split32(m8[...])
    moved = dot(jnp.concatenate([high, low], axis=0).astype(BF16), pm[...])
    mixed = moved[0:8] + moved[8:16]
    for cg in range(4):
        s4[cg] = mixed[0:4, cg * 128 : cg * 128 + 128]

    @pl.loop(1, GY)
    def _(s):
        t = (j + s) % GY
        remote(s4.at[t // 4], r4.at[j], 3, (i, t)).start()

    r4[j] = s4[yy]

    @pl.when(i > 0)
    def _():
        up_x.wait_recv()

    @pl.when(i < GX - 1)
    def _():
        down_x.wait_recv()

    z_of = lane % 64

    def shifted(value, d):
        if d == 0:
            return jnp.where(z_of == 0, 0.0, pltpu.roll(value, 1, axis=1))
        if d == 2:
            return jnp.where(z_of == 63, 0.0, pltpu.roll(value, 127, axis=1))
        return value

    def columns(value, buffer, base):
        for d in range(3):
            buffer[base + d * 36 : base + d * 36 + 36, :] = shifted(value, d)[0:36]
        return split(buffer[base : base + KB, :])

    stage[...] = jnp.zeros_like(stage)
    stage2[...] = jnp.zeros_like(stage2)

    @pl.loop(0, 8)
    def _(x):
        for u in range(7):
            near = t2[rows((x * 12 + u) * 24, 24), :]
            far = t2[rows((x * 12 + u + 5) * 24, 24), :]
            even = jnp.where(first_half, near, pltpu.roll(far, 64, axis=1))
            odd = jnp.where(first_half, pltpu.roll(near, 64, axis=1), far)
            cc[pl.ds(u * 40, 18, stride=2), :] = even[0:18]
            cc[pl.ds(u * 40 + 1, 18, stride=2), :] = odd[0:18]
            high, low = columns(cc[u * 40 : u * 40 + 40, :], stage, u * KB)
            for b in range(3):
                v = u - b
                if 0 <= v < 5:
                    place = pl.ds(pl.multiple_of(x * 336 + b * KB, 16), KB)
                    ubh[place, v * 128 : v * 128 + 128] = high
                    ubl[place, v * 128 : v * 128 + 128] = low

    w1 = wst1[...].astype(BF16)
    wide_lane = lax.broadcasted_iota(jnp.int32, (1, 640), 1)
    keep_y = jnp.where((wide_lane < 64) & (j == 0), 0.0, 1.0) * jnp.where(
        (wide_lane >= 576) & (j == GY - 1), 0.0, 1.0
    )

    @pl.loop(0, 6)
    def _(x):
        place = pl.ds(pl.multiple_of(x * 336, 16), 1008)
        res = dot(w1, ubh[place, :])
        value = res[0:40] + res[40:80] + dot(w1[0:40], ubl[place, :])
        outside = ((x == 0) & (i == 0)) | ((x == 5) & (i == GX - 1))
        keep = keep_y * jnp.where(outside, 0.0, 1.0)
        hid[rows(x * 40, 40), :] = gelu(value) * keep

    wait_recv(r4, GY - 1, 3)
    l_d4.wait()
    modes = jnp.concatenate(
        [jnp.concatenate([r4[:, b * 2 + part, :] for b in range(2)], axis=0) for part in range(2)], axis=1
    )
    result = combine(dot(d4[...], tripled(modes)), -1.0)
    for part in range(2):
        for y in range(4):
            s5[pl.ds(part * 4 + y, 8, stride=8), :] = result[part][y * 8 : y * 8 + 8]

    @pl.loop(1, GX)
    def _(s):
        t = (i + s) % GX
        row = (t // 8) * 2 + t % 2
        remote(s5.at[rows(row * 8, 8)], r5.at[rows(i * 8, 8)], 4, (t, j)).start()

    r5[rows(i * 8, 8), :] = s5[rows(l * 8, 8), :]

    @pl.loop(0, 6)
    def _(x):
        pairs = [hid[rows(x * 40, 40), v * 128 : v * 128 + 128] for v in range(5)]
        units = [(pairs[n], [(b, n - b) for b in range(3) if 0 <= n - b < 3]) for n in range(5)]
        units.append((jnp.where(first_half, pairs[3], pltpu.roll(pairs[4], 64, axis=1)), [(0, 3)]))
        units.append((jnp.where(first_half, pairs[4], pairs[0]), [(1, 3)]))
        units.append((jnp.where(first_half, pltpu.roll(pairs[0], 64, axis=1), pairs[1]), [(2, 3)]))
        for n, (value, places) in enumerate(units):
            high, low = columns(value, stage2, n * KB)
            for b, v in places:
                place = pl.ds(pl.multiple_of(x * 336 + b * KB, 16), KB)
                ub2h[place, v * 128 : v * 128 + 128] = high
                ub2l[place, v * 128 : v * 128 + 128] = low

    wait_recv(r5, 31 * 8, 4)
    l_d5.wait()
    result = combine(dot(d5[...], tripled(gathered(r5))), -1.0)
    for part in range(2):
        for y in range(4):
            s6[pl.ds(y * 64 + part, 32, stride=2), :] = result[part][:, y * 128 : y * 128 + 128]

    @pl.loop(1, 32)
    def _(s):
        n = (slot + s) % 32
        remote(s6.at[rows(n * 8, 8)], r6.at[rows(slot * 8, 8)], 5, peer(n % 8, n // 8)).start()

    r6[rows(slot * 8, 8), :] = s6[rows(slot * 8, 8), :]

    w2 = wst2[...].astype(BF16)

    @pl.loop(0, NX)
    def _(x):
        place = pl.ds(pl.multiple_of(x * 336, 16), 1008)
        res = dot(w2, ub2h[place, :])
        value = res[0:40] + res[40:80] + dot(w2[0:40], ub2l[place, :])
        for v in range(4):
            ct[v * 40 : v * 40 + 40, :] = value[:, v * 128 : v * 128 + 128]
        for v in range(4):
            even = ct[pl.ds(v * 40, 18, stride=2), :]
            odd = ct[pl.ds(v * 40 + 1, 18, stride=2), :]
            near = jnp.where(first_half, even, pltpu.roll(odd, 64, axis=1))
            far = jnp.where(first_half, pltpu.roll(even, 64, axis=1), odd)
            y_near, y_far = (v, v + 5) if v < 3 else (3, 4)
            n2[y_near * 24 : y_near * 24 + 18, :] = near
            n2[y_far * 24 : y_far * 24 + 18, :] = far
        for m in range(18):
            co[rows(x * 8, 8), m * 128 : m * 128 + 128] = n2[pl.ds(m, 8, stride=24), :]

    wait_recv(r6, 31 * 8, 5)
    l_fi.wait()
    results = []
    for e in range(2):
        left = jnp.concatenate(
            [
                jnp.concatenate(
                    [
                        jnp.concatenate(
                            [r6[pl.ds((2 * h + e) * 64 + x * 2 + part, 8, stride=8), :] for x in range(NX)], axis=0
                        )
                        for part in range(2)
                    ],
                    axis=1,
                )
                for h in range(2)
            ],
            axis=0,
        )
        high, low = split(left)
        results.append(dot(high, fi[e, 0]) + dot(low, fi[e, 0]) + dot(high, fi[e, 1]))
    for h in range(2):
        one, two = results[0][h * 32 : h * 32 + 32], results[1][h * 32 : h * 32 + 32]
        spectral = jnp.concatenate([one[:, :512], one[:, 512:] + two[:, :128], two[:, 128:]], axis=1)
        full = spectral + co[:, h * 1152 : h * 1152 + 1152]
        for x in range(NX):
            out_ref[x, :, h * 1152 : h * 1152 + 1152] = full[x * 8 : x * 8 + 8]

    wait_send(s1, 31 * 8, 0)
    wait_send(s2, 31 * 8, 1)
    wait_send(r3, GY - 1, 2)
    wait_send(r4, GY - 1, 3)
    wait_send(r5, 31 * 8, 4)
    wait_send(s6, 31 * 8, 5)

    @pl.when(j > 0)
    def _():
        down_y.wait_send()

    @pl.when(j < GY - 1)
    def _():
        up_y.wait_send()

    @pl.when(i > 0)
    def _():
        down_x.wait_send()

    @pl.when(i < GX - 1)
    def _():
        up_x.wait_send()


def on_device(state_field, conv_first, conv_second, spec_real, spec_imag):
    constants = [jnp.asarray(t) for t in tables()]
    vm = pltpu.VMEM
    scratch = [
        vm((NX, NY, C * Z), F32), vm((3, 3, C, 3 * C), F32), vm((3, 3, C, 3 * C), F32),
        vm((C, 2, MZ * C), F32), vm((C, 2, MZ * C), F32),
        vm((2, 704, 256), BF16), vm((64, 96), BF16), vm((64, 96), BF16), vm((64, 96), BF16), vm((64, 96), BF16),
        vm((4, 40, 128), F32), vm((128, 512), BF16), vm((512, 512), BF16), vm((2, 2, 256, 640), BF16),
        vm((256, 128), F32), vm((256, 128), F32), vm((256, 128), F32), vm((256, 128), F32),
        vm((GY, 4, 128), F32), vm((GY, 4, 128), F32), vm((4, 4, 128), F32), vm((GY, 4, 128), F32),
        vm((64, 128), F32), vm((256, 128), F32), vm((256, 128), F32), vm((256, 128), F32),
        vm((8, 12, 24, 128), F32), vm((8, 512), F32), vm((80, 9 * KB), F32), vm((80, 9 * KB), F32),
        vm((280, 128), F32), vm((7 * KB, 128), F32), vm((8 * 336, 640), BF16), vm((8 * 336, 640), BF16),
        vm((240, 640), F32), vm((8 * KB, 128), F32), vm((6 * 336, 512), BF16), vm((6 * 336, 512), BF16),
        vm((160, 128), F32), vm((192, 128), F32), vm((32, C * Z), F32),
        pltpu.SemaphoreType.DMA((14,)), pltpu.SemaphoreType.DMA((6,)), pltpu.SemaphoreType.DMA((6,)),
        pltpu.SemaphoreType.DMA((4,)), pltpu.SemaphoreType.DMA((4,)),
    ]
    before = pl.pallas_call(
        kernel,
        out_shape=jax.ShapeDtypeStruct((NX, NY, C * Z), F32),
        in_specs=[pl.BlockSpec(memory_space=pl.ANY)] * (5 + len(constants)),
        out_specs=pl.BlockSpec(memory_space=pltpu.VMEM),
        scratch_shapes=scratch,
        compiler_params=pltpu.CompilerParams(
            collective_id=0, has_side_effects=True, vmem_limit_bytes=56 * 1024 * 1024
        ),
    )(
        state_field, conv_first, conv_second,
        jnp.transpose(spec_real[0], (1, 0, 2)), jnp.transpose(spec_imag[0], (1, 0, 2)), *constants
    )
    return jax.nn.gelu(before, approximate=False)


def solution(mesh):
    in_specs = (P("gx", "gy", None), P(), P(), P("gx", "gy", None, None), P("gx", "gy", None, None))
    return jax.shard_map(
        on_device, mesh=mesh, in_specs=in_specs, out_specs=P("gx", "gy", None), check_vma=False
    )
```

```python
import jax
import jax.numpy as jnp
import numpy as np
from jax import lax
from jax.experimental import pallas as pl
from jax.experimental.pallas import tpu as pltpu
from jax.sharding import PartitionSpec as P

C = 36
Z = 64
MZ = 12
X = 128
Y = 128
GX = 32
GY = 16
NX = 4
NY = 8
GROUP = 8
KB = 112
F32 = jnp.float32
BF16 = jnp.bfloat16
MESH = pl.DeviceIdType.MESH


def halves(table):
    high = table.astype(jnp.bfloat16)
    low = (table - high.astype(np.float64)).astype(jnp.bfloat16)
    return high, low


def stacked(table):
    high, low = halves(table)
    return np.concatenate([high, high, low], axis=-1)


def tables():
    r = np.arange(MZ)
    z = np.arange(Z)
    zr = 2 * np.pi * np.outer(z, r) / Z
    forward = np.zeros((704, 256))
    backward = np.zeros((2, 256, 640))
    weight = np.where(r == 0, 1.0, 2.0) / (X * Y * Z)
    for c in range(9):
        rows = slice(64 + c * Z, 64 + c * Z + Z)
        forward[rows, c * MZ : c * MZ + MZ] = np.cos(zr)
        forward[rows, 128 + c * MZ : 128 + c * MZ + MZ] = -np.sin(zr)
        for e in range(2):
            cols = slice(64 * e + c * Z, 64 * e + c * Z + Z)
            backward[e, c * MZ : c * MZ + MZ, cols] = (np.cos(zr) * weight).T
            backward[e, 128 + c * MZ : 128 + c * MZ + MZ, cols] = -(np.sin(zr) * weight).T
    freq = np.where(np.arange(32) < 16, np.arange(32), np.arange(32) + 96)

    def pair(first, second):
        angle = 2 * np.pi * (np.outer(first, second) % 128) / 128
        return np.concatenate([np.cos(angle), np.sin(angle)], axis=0)

    members = np.array([[(t // 2) * 8 + g * 2 + t % 2 for t in range(GROUP)] for g in range(4)])
    xs = [(members[g][:, None] * NX + np.arange(NX)[None, :]).reshape(32) for g in range(4)]
    blocks = np.arange(4) * 4
    ys = [((blocks[:, None] + g) * NY + np.arange(NY)[None, :]).reshape(32) for g in range(4)]
    halved = np.concatenate([freq[0::2], freq[1::2]])
    d1 = stacked(np.stack([pair(freq, v) for v in xs]))
    d2 = stacked(np.stack([pair(halved, v) for v in ys]))
    d4 = stacked(np.stack([pair(v, halved) for v in ys]))
    d5 = stacked(np.stack([pair(v, freq) for v in xs]))
    mask = np.zeros((4, 40, 128), np.float32)
    spread = np.zeros((128, 512))
    order = np.zeros((512, 512))
    for c in range(C):
        mask[c // 9, c, (c % 9) * MZ : (c % 9) * MZ + MZ] = 1
    for c in range(9):
        for k in range(MZ):
            spread[c * MZ + k, k * C : k * C + C] = 1
    for k in range(MZ):
        for o in range(C):
            order[k * C + o, (o // 9) * 128 + (o % 9) * MZ + k] = 1
    return (
        np.stack(halves(forward)),
        d1,
        d2,
        d4,
        d5,
        mask,
        spread.astype(jnp.bfloat16),
        order.astype(jnp.bfloat16),
        np.stack(halves(backward), axis=1),
    )


def split(value):
    high = value.astype(BF16)
    low = (value - high.astype(F32)).astype(BF16)
    return high, low


def split32(value):
    high = value.astype(BF16).astype(F32)
    return high, value - high


def dot(left, right):
    return jnp.dot(left, right, preferred_element_type=F32)


def gelu(value):
    return 0.5 * value * (1.0 + lax.erf(value * 0.7071067811865476))


def kernel(
    state_hbm, wf_hbm, ws_hbm, sr_hbm, si_hbm,
    fz_hbm, d1_hbm, d2_hbm, d4_hbm, d5_hbm, mk_hbm, ex_hbm, pm_hbm, fi_hbm,
    out_ref,
    st, wf, ws, sr, si, fz, d1, d2, d4, d5, mk, ex, pm, fi,
    s1, r1, s2, r2, s3, r3, s4, r4, s5, r5, s6, r6,
    tt, m8, wst1, wst2, cc, stage, ubh, ubl, hid, stage2, ub2h, ub2l, ct, n2, co,
    load_sem, send_sem, recv_sem, halo_send, halo_recv, ready_sem,
):
    i = lax.axis_index("gx")
    j = lax.axis_index("gy")
    g = (i % 8) // 2
    l = (i // 8) * 2 + i % 2
    yy = j // 4
    zz = j % 4

    sources = [
        (state_hbm, st), (fz_hbm, fz), (d1_hbm.at[g], d1), (d2_hbm.at[zz], d2), (wf_hbm, wf),
        (ws_hbm, ws), (sr_hbm, sr), (si_hbm, si), (mk_hbm, mk), (ex_hbm, ex),
        (pm_hbm, pm), (d4_hbm.at[zz], d4), (d5_hbm.at[g], d5), (fi_hbm, fi),
    ]
    loads = [pltpu.make_async_copy(src, dst, load_sem.at[n]) for n, (src, dst) in enumerate(sources)]
    loads[0].start()
    loads[1].start()
    (l_st, l_fz, l_d1, l_d2, l_wf, l_ws, l_sr, l_si, l_mk, l_ex, l_pm, l_d4, l_d5, l_fi) = loads

    def peer(t, y):
        return ((t // 2) * 8 + g * 2 + t % 2, y * 4 + zz)

    barrier = pltpu.get_barrier_semaphore()

    across = [(i, yy * 4 + (zz + 1) % 4), (i, yy * 4 + (zz + 3) % 4)]
    for device in across:
        pl.semaphore_signal(barrier, inc=1, device_id=device, device_id_type=MESH)

    above = (zz == 3) & (j < GY - 1)
    below = (zz == 0) & (j > 0)

    @pl.when(above)
    def _():
        pl.semaphore_signal(barrier, inc=1, device_id=(i, (j + 1) % GY), device_id_type=MESH)

    @pl.when(below)
    def _():
        pl.semaphore_signal(barrier, inc=1, device_id=(i, (j + GY - 1) % GY), device_id_type=MESH)

    @pl.loop(1, GROUP)
    def _(s):
        for n in range(1, 4):
            pl.semaphore_signal(
                barrier, inc=1, device_id=peer((l + s) % GROUP, (yy + n) % 4), device_id_type=MESH
            )

    for n in range(1, 4):
        pl.semaphore_signal(barrier, inc=1, device_id=peer(l, (yy + n) % 4), device_id_type=MESH)


    @pl.loop(1, GX)
    def _(s):
        pl.semaphore_signal(barrier, inc=1, device_id=((i + s) % GX, j), device_id_type=MESH)

    def remote(src, dst, stage_no, device):
        return pltpu.make_async_remote_copy(
            src_ref=src, dst_ref=dst, send_sem=send_sem.at[stage_no], recv_sem=recv_sem.at[stage_no],
            device_id=device, device_id_type=MESH,
        )

    def rows(start, size):
        return pl.ds(pl.multiple_of(start, 8), size)

    def wait_recv(buffer, count, stage_no):
        part = buffer.at[pl.ds(0, count)]
        pltpu.make_async_copy(part, part, recv_sem.at[stage_no]).wait()

    def wait_send(buffer, count, stage_no):
        part = buffer.at[pl.ds(0, count)]
        pltpu.make_async_copy(part, part, send_sem.at[stage_no]).wait()

    lane = lax.broadcasted_iota(jnp.int32, (1, 128), 1)
    first_half = lane < 64

    l_st.wait()
    l_fz.wait()
    field = st[...].reshape(NX * NY, C * Z)
    for e in range(2):
        left = jnp.concatenate([field[:, h * 1152 + e * 512 : h * 1152 + e * 512 + 640] for h in range(2)], axis=0)
        high, low = split(left)
        fh = fz[0, 64 * (1 - e) : 64 * (1 - e) + 640, :]
        fl = fz[1, 64 * (1 - e) : 64 * (1 - e) + 640, :]
        res = dot(high, fh) + dot(low, fh) + dot(high, fl)
        for h in range(2):
            for part in range(2):
                for x in range(NX):
                    s1[pl.ds((2 * h + e) * 64 + x * 2 + part, 8, stride=8), :] = res[
                        h * 32 + x * 8 : h * 32 + x * 8 + 8, part * 128 : part * 128 + 128
                    ]
    near = GX - 1 + 24 + 2
    pl.semaphore_wait(barrier, jnp.where(above | below, near + 1, near))
    slot = yy * 8 + l

    @pl.loop(1, 32)
    def _(s):
        n = (slot + s) % 32
        remote(s1.at[rows(n * 8, 8)], r1.at[rows(slot * 8, 8)], 0, peer(n % 8, n // 8)).start()

    r1[rows(slot * 8, 8), :] = s1[rows(slot * 8, 8), :]
    for load in loads[2:]:
        load.start()

    cc[...] = jnp.zeros_like(cc)
    t2 = tt.reshape(8 * 12 * 24, 128)
    for x in range(NX):
        for m in range(18):
            t2[pl.ds(((x + 2) * 12 + 2) * 24 + m, 8, stride=24), :] = st[x, :, m * 128 : (m + 1) * 128]

    def halo(n, src, dst, device):
        return pltpu.make_async_remote_copy(
            src_ref=src, dst_ref=dst, send_sem=halo_send.at[n], recv_sem=halo_recv.at[n],
            device_id=device, device_id_type=MESH,
        )

    down_y = halo(0, tt.at[2:6, 2:4], tt.at[2:6, 10:12], (i, (j + GY - 1) % GY))
    up_y = halo(1, tt.at[2:6, 8:10], tt.at[2:6, 0:2], (i, (j + 1) % GY))
    down_x = halo(2, tt.at[2:4], tt.at[6:8], ((i + GX - 1) % GX, j))
    up_x = halo(3, tt.at[4:6], tt.at[0:2], ((i + 1) % GX, j))

    @pl.when(j == 0)
    def _():
        tt[2:6, 0:2] = jnp.zeros((4, 2, 24, 128), F32)

    @pl.when(j == GY - 1)
    def _():
        tt[2:6, 10:12] = jnp.zeros((4, 2, 24, 128), F32)

    @pl.when(i == 0)
    def _():
        tt[0:2] = jnp.zeros((2, 12, 24, 128), F32)

    @pl.when(i == GX - 1)
    def _():
        tt[6:8] = jnp.zeros((2, 12, 24, 128), F32)

    def filters(src, scratch):
        scratch[...] = jnp.zeros_like(scratch)
        for tap_x in range(3):
            for tap_y in range(3):
                tap = tap_x * 3 + tap_y
                high, low = split32(src[tap_x, tap_y])
                scratch[0:36, tap * KB : tap * KB + 108] = high
                scratch[40:76, tap * KB : tap * KB + 108] = low

    @pl.when(j > 0)
    def _():
        down_y.start()

    @pl.when(j < GY - 1)
    def _():
        up_y.start()

    l_wf.wait()
    filters(wf, wst1)

    wait_recv(r1, 31 * 8, 0)
    for device in across:
        pl.semaphore_signal(ready_sem, inc=1, device_id=device, device_id_type=MESH)
    l_d1.wait()

    def gathered(buffer):
        return jnp.concatenate([buffer[pl.ds(k, 32, stride=8), :] for k in range(8)], axis=1)

    def tripled(value):
        high, low = split(value)
        return jnp.concatenate([high, low, high], axis=0)

    def exchanged(buffer):
        return jnp.concatenate(
            [buffer[pl.ds(y * 64 + part, 32, stride=2), :] for part in range(2) for y in range(4)], axis=1
        )

    def combine(res, sign):
        half = res.shape[1] // 2
        top, bottom = res[:32], res[32:]
        real = top[:, :half] + sign * bottom[:, half:]
        imag = top[:, half:] - sign * bottom[:, :half]
        return real, imag

    real, imag = combine(dot(d1[...], tripled(exchanged(r1))), 1.0)
    for k in range(4):
        s2[pl.ds(k, 32, stride=8), :] = real[:, k * 128 : k * 128 + 128]
        s2[pl.ds(k + 4, 32, stride=8), :] = imag[:, k * 128 : k * 128 + 128]

    @pl.loop(1, GX)
    def _(s):
        t = (i + s) % GX
        remote(s2.at[rows(t * 8, 8)], r2.at[rows((g * 8 + l) * 8, 8)], 1, (t, j)).start()

    r2[rows((g * 8 + l) * 8, 8), :] = s2[rows(i * 8, 8), :]
    l_ws.wait()
    filters(ws, wst2)

    wait_recv(r2, 31 * 8, 1)
    l_d2.wait()
    parts = []
    for part in range(2):
        column = []
        for y in range(4):
            k = part * 4 + y
            terms = [r2[pl.ds(n * 64 + k, 8, stride=8), :] for n in range(4)]
            column.append((terms[0] + terms[1]) + (terms[2] + terms[3]))
        parts.append(jnp.concatenate(column, axis=0))
    result = combine(dot(d2[...], tripled(jnp.concatenate(parts, axis=1))), 1.0)
    for b in range(2):
        for part in range(2):
            s3[:, b * 2 + part, :] = result[part][b * 16 : b * 16 + 16]

    pl.semaphore_wait(ready_sem, 2)

    @pl.loop(1, GY)
    def _(s):
        t = (j + s) % GY
        remote(s3.at[t], r3.at[j], 2, (i, t)).start()

    r3[j] = s3[j]

    @pl.when(j > 0)
    def _():
        up_y.wait_recv()

    @pl.when(j < GY - 1)
    def _():
        down_y.wait_recv()

    @pl.when(i > 0)
    def _():
        down_x.start()

    @pl.when(i < GX - 1)
    def _():
        up_x.start()

    wait_recv(r3, GY - 1, 2)
    total = [(r3[4 * n] + r3[4 * n + 1]) + (r3[4 * n + 2] + r3[4 * n + 3]) for n in range(4)]
    for load in (l_mk, l_ex, l_sr, l_si, l_pm):
        load.wait()
    placed = []
    for q in range(2):
        for part in range(2):
            acc = None
            for cg in range(4):
                n = q * 2 + part
                term = total[cg][n : n + 1, :] * mk[cg]
                acc = term if acc is None else acc + term
            placed.append(acc)
    high, low = split(jnp.concatenate(placed, axis=0))
    wide = dot(high, ex[...]) + dot(low, ex[...])
    m8[...] = jnp.zeros_like(m8)
    for q in range(2):
        c_re = wide[q * 80 : q * 80 + 36, :432]
        c_im = wide[q * 80 + 40 : q * 80 + 76, :432]
        w_re, w_im = sr[:, q, :], si[:, q, :]
        m8[2 * q : 2 * q + 1, 0:432] = jnp.sum(c_re * w_re - c_im * w_im, axis=0, keepdims=True)
        m8[2 * q + 1 : 2 * q + 2, 0:432] = jnp.sum(c_re * w_im + c_im * w_re, axis=0, keepdims=True)
    high, low = split32(m8[...])
    moved = dot(jnp.concatenate([high, low], axis=0).astype(BF16), pm[...])
    mixed = moved[0:8] + moved[8:16]
    for cg in range(4):
        s4[cg] = mixed[0:4, cg * 128 : cg * 128 + 128]

    @pl.loop(1, GY)
    def _(s):
        t = (j + s) % GY
        remote(s4.at[t // 4], r4.at[j], 3, (i, t)).start()

    r4[j] = s4[yy]

    @pl.when(i > 0)
    def _():
        up_x.wait_recv()

    @pl.when(i < GX - 1)
    def _():
        down_x.wait_recv()

    z_of = lane % 64

    def shifted(value, d):
        if d == 0:
            return jnp.where(z_of == 0, 0.0, pltpu.roll(value, 1, axis=1))
        if d == 2:
            return jnp.where(z_of == 63, 0.0, pltpu.roll(value, 127, axis=1))
        return value

    def columns(value, buffer, base):
        for d in range(3):
            buffer[base + d * 36 : base + d * 36 + 36, :] = shifted(value, d)[0:36]
        return split(buffer[base : base + KB, :])

    stage[...] = jnp.zeros_like(stage)
    stage2[...] = jnp.zeros_like(stage2)

    @pl.loop(0, 8)
    def _(x):
        for u in range(7):
            near = t2[rows((x * 12 + u) * 24, 24), :]
            far = t2[rows((x * 12 + u + 5) * 24, 24), :]
            even = jnp.where(first_half, near, pltpu.roll(far, 64, axis=1))
            odd = jnp.where(first_half, pltpu.roll(near, 64, axis=1), far)
            cc[pl.ds(u * 40, 18, stride=2), :] = even[0:18]
            cc[pl.ds(u * 40 + 1, 18, stride=2), :] = odd[0:18]
            high, low = columns(cc[u * 40 : u * 40 + 40, :], stage, u * KB)
            for b in range(3):
                v = u - b
                if 0 <= v < 5:
                    place = pl.ds(pl.multiple_of(x * 336 + b * KB, 16), KB)
                    ubh[place, v * 128 : v * 128 + 128] = high
                    ubl[place, v * 128 : v * 128 + 128] = low

    w1 = wst1[...].astype(BF16)
    wide_lane = lax.broadcasted_iota(jnp.int32, (1, 640), 1)
    keep_y = jnp.where((wide_lane < 64) & (j == 0), 0.0, 1.0) * jnp.where(
        (wide_lane >= 576) & (j == GY - 1), 0.0, 1.0
    )

    @pl.loop(0, 6)
    def _(x):
        place = pl.ds(pl.multiple_of(x * 336, 16), 1008)
        res = dot(w1, ubh[place, :])
        value = res[0:40] + res[40:80] + dot(w1[0:40], ubl[place, :])
        outside = ((x == 0) & (i == 0)) | ((x == 5) & (i == GX - 1))
        keep = keep_y * jnp.where(outside, 0.0, 1.0)
        hid[rows(x * 40, 40), :] = gelu(value) * keep

    wait_recv(r4, GY - 1, 3)
    l_d4.wait()
    modes = jnp.concatenate(
        [jnp.concatenate([r4[:, b * 2 + part, :] for b in range(2)], axis=0) for part in range(2)], axis=1
    )
    result = combine(dot(d4[...], tripled(modes)), -1.0)
    for part in range(2):
        for y in range(4):
            s5[pl.ds(part * 4 + y, 8, stride=8), :] = result[part][y * 8 : y * 8 + 8]

    @pl.loop(1, GX)
    def _(s):
        t = (i + s) % GX
        row = (t // 8) * 2 + t % 2
        remote(s5.at[rows(row * 8, 8)], r5.at[rows(i * 8, 8)], 4, (t, j)).start()

    r5[rows(i * 8, 8), :] = s5[rows(l * 8, 8), :]

    @pl.loop(0, 6)
    def _(x):
        pairs = [hid[rows(x * 40, 40), v * 128 : v * 128 + 128] for v in range(5)]
        units = [(pairs[n], [(b, n - b) for b in range(3) if 0 <= n - b < 3]) for n in range(5)]
        units.append((jnp.where(first_half, pairs[3], pltpu.roll(pairs[4], 64, axis=1)), [(0, 3)]))
        units.append((jnp.where(first_half, pairs[4], pairs[0]), [(1, 3)]))
        units.append((jnp.where(first_half, pltpu.roll(pairs[0], 64, axis=1), pairs[1]), [(2, 3)]))
        for n, (value, places) in enumerate(units):
            high, low = columns(value, stage2, n * KB)
            for b, v in places:
                place = pl.ds(pl.multiple_of(x * 336 + b * KB, 16), KB)
                ub2h[place, v * 128 : v * 128 + 128] = high
                ub2l[place, v * 128 : v * 128 + 128] = low

    wait_recv(r5, 31 * 8, 4)
    l_d5.wait()
    result = combine(dot(d5[...], tripled(gathered(r5))), -1.0)
    for part in range(2):
        for y in range(4):
            s6[pl.ds(y * 64 + part, 32, stride=2), :] = result[part][:, y * 128 : y * 128 + 128]

    @pl.loop(1, 32)
    def _(s):
        n = (slot + s) % 32
        remote(s6.at[rows(n * 8, 8)], r6.at[rows(slot * 8, 8)], 5, peer(n % 8, n // 8)).start()

    r6[rows(slot * 8, 8), :] = s6[rows(slot * 8, 8), :]

    w2 = wst2[...].astype(BF16)

    @pl.loop(0, NX)
    def _(x):
        place = pl.ds(pl.multiple_of(x * 336, 16), 1008)
        res = dot(w2, ub2h[place, :])
        value = res[0:40] + res[40:80] + dot(w2[0:40], ub2l[place, :])
        for v in range(4):
            ct[v * 40 : v * 40 + 40, :] = value[:, v * 128 : v * 128 + 128]
        for v in range(4):
            even = ct[pl.ds(v * 40, 18, stride=2), :]
            odd = ct[pl.ds(v * 40 + 1, 18, stride=2), :]
            near = jnp.where(first_half, even, pltpu.roll(odd, 64, axis=1))
            far = jnp.where(first_half, pltpu.roll(even, 64, axis=1), odd)
            y_near, y_far = (v, v + 5) if v < 3 else (3, 4)
            n2[y_near * 24 : y_near * 24 + 18, :] = near
            n2[y_far * 24 : y_far * 24 + 18, :] = far
        for m in range(18):
            co[rows(x * 8, 8), m * 128 : m * 128 + 128] = n2[pl.ds(m, 8, stride=24), :]

    wait_recv(r6, 31 * 8, 5)
    l_fi.wait()
    results = []
    for e in range(2):
        left = jnp.concatenate(
            [
                jnp.concatenate(
                    [
                        jnp.concatenate(
                            [r6[pl.ds((2 * h + e) * 64 + x * 2 + part, 8, stride=8), :] for x in range(NX)], axis=0
                        )
                        for part in range(2)
                    ],
                    axis=1,
                )
                for h in range(2)
            ],
            axis=0,
        )
        high, low = split(left)
        results.append(dot(high, fi[e, 0]) + dot(low, fi[e, 0]) + dot(high, fi[e, 1]))
    for h in range(2):
        one, two = results[0][h * 32 : h * 32 + 32], results[1][h * 32 : h * 32 + 32]
        spectral = jnp.concatenate([one[:, :512], one[:, 512:] + two[:, :128], two[:, 128:]], axis=1)
        full = spectral + co[:, h * 1152 : h * 1152 + 1152]
        for x in range(NX):
            out_ref[x, :, h * 1152 : h * 1152 + 1152] = full[x * 8 : x * 8 + 8]

    wait_send(s1, 31 * 8, 0)
    wait_send(s2, 31 * 8, 1)
    wait_send(r3, GY - 1, 2)
    wait_send(r4, GY - 1, 3)
    wait_send(r5, 31 * 8, 4)
    wait_send(s6, 31 * 8, 5)

    @pl.when(j > 0)
    def _():
        down_y.wait_send()

    @pl.when(j < GY - 1)
    def _():
        up_y.wait_send()

    @pl.when(i > 0)
    def _():
        down_x.wait_send()

    @pl.when(i < GX - 1)
    def _():
        up_x.wait_send()


def on_device(state_field, conv_first, conv_second, spec_real, spec_imag):
    constants = [jnp.asarray(t) for t in tables()]
    vm = pltpu.VMEM
    scratch = [
        vm((NX, NY, C * Z), F32), vm((3, 3, C, 3 * C), F32), vm((3, 3, C, 3 * C), F32),
        vm((C, 2, MZ * C), F32), vm((C, 2, MZ * C), F32),
        vm((2, 704, 256), BF16), vm((64, 96), BF16), vm((64, 96), BF16), vm((64, 96), BF16), vm((64, 96), BF16),
        vm((4, 40, 128), F32), vm((128, 512), BF16), vm((512, 512), BF16), vm((2, 2, 256, 640), BF16),
        vm((256, 128), F32), vm((256, 128), F32), vm((256, 128), F32), vm((256, 128), F32),
        vm((GY, 4, 128), F32), vm((GY, 4, 128), F32), vm((4, 4, 128), F32), vm((GY, 4, 128), F32),
        vm((64, 128), F32), vm((256, 128), F32), vm((256, 128), F32), vm((256, 128), F32),
        vm((8, 12, 24, 128), F32), vm((8, 512), F32), vm((80, 9 * KB), F32), vm((80, 9 * KB), F32),
        vm((280, 128), F32), vm((7 * KB, 128), F32), vm((8 * 336, 640), BF16), vm((8 * 336, 640), BF16),
        vm((240, 640), F32), vm((8 * KB, 128), F32), vm((6 * 336, 512), BF16), vm((6 * 336, 512), BF16),
        vm((160, 128), F32), vm((192, 128), F32), vm((32, C * Z), F32),
        pltpu.SemaphoreType.DMA((14,)), pltpu.SemaphoreType.DMA((6,)), pltpu.SemaphoreType.DMA((6,)),
        pltpu.SemaphoreType.DMA((4,)), pltpu.SemaphoreType.DMA((4,)), pltpu.SemaphoreType.REGULAR,
    ]
    before = pl.pallas_call(
        kernel,
        out_shape=jax.ShapeDtypeStruct((NX, NY, C * Z), F32),
        in_specs=[pl.BlockSpec(memory_space=pl.ANY)] * (5 + len(constants)),
        out_specs=pl.BlockSpec(memory_space=pltpu.VMEM),
        scratch_shapes=scratch,
        compiler_params=pltpu.CompilerParams(
            collective_id=0, has_side_effects=True, vmem_limit_bytes=56 * 1024 * 1024
        ),
    )(
        state_field, conv_first, conv_second,
        jnp.transpose(spec_real[0], (1, 0, 2)), jnp.transpose(spec_imag[0], (1, 0, 2)), *constants
    )
    return jax.nn.gelu(before, approximate=False)


def solution(mesh):
    in_specs = (P("gx", "gy", None), P(), P(), P("gx", "gy", None, None), P("gx", "gy", None, None))
    return jax.shard_map(
        on_device, mesh=mesh, in_specs=in_specs, out_specs=P("gx", "gy", None), check_vma=False
    )
```

```python
import jax
import jax.numpy as jnp
import numpy as np
from jax import lax
from jax.experimental import pallas as pl
from jax.experimental.pallas import tpu as pltpu
from jax.sharding import PartitionSpec as P

C = 36
Z = 64
MZ = 12
X = 128
Y = 128
GX = 32
GY = 16
NX = 4
NY = 8
GROUP = 8
KB = 112
F32 = jnp.float32
BF16 = jnp.bfloat16
MESH = pl.DeviceIdType.MESH


def halves(table):
    high = table.astype(jnp.bfloat16)
    low = (table - high.astype(np.float64)).astype(jnp.bfloat16)
    return high, low


def stacked(table):
    high, low = halves(table)
    return np.concatenate([high, high, low], axis=-1)


def tables():
    r = np.arange(MZ)
    z = np.arange(Z)
    zr = 2 * np.pi * np.outer(z, r) / Z
    forward = np.zeros((704, 256))
    backward = np.zeros((2, 256, 640))
    weight = np.where(r == 0, 1.0, 2.0) / (X * Y * Z)
    for c in range(9):
        rows = slice(64 + c * Z, 64 + c * Z + Z)
        forward[rows, c * MZ : c * MZ + MZ] = np.cos(zr)
        forward[rows, 128 + c * MZ : 128 + c * MZ + MZ] = -np.sin(zr)
        for e in range(2):
            cols = slice(64 * e + c * Z, 64 * e + c * Z + Z)
            backward[e, c * MZ : c * MZ + MZ, cols] = (np.cos(zr) * weight).T
            backward[e, 128 + c * MZ : 128 + c * MZ + MZ, cols] = -(np.sin(zr) * weight).T
    freq = np.where(np.arange(32) < 16, np.arange(32), np.arange(32) + 96)

    def pair(first, second):
        angle = 2 * np.pi * (np.outer(first, second) % 128) / 128
        return np.concatenate([np.cos(angle), np.sin(angle)], axis=0)

    members = np.array([[(t // 2) * 8 + g * 2 + t % 2 for t in range(GROUP)] for g in range(4)])
    xs = [(members[g][:, None] * NX + np.arange(NX)[None, :]).reshape(32) for g in range(4)]
    blocks = np.arange(4) * 4
    ys = [((blocks[:, None] + g) * NY + np.arange(NY)[None, :]).reshape(32) for g in range(4)]
    halved = np.concatenate([freq[0::2], freq[1::2]])
    d1 = stacked(np.stack([pair(freq, v) for v in xs]))
    d2 = stacked(np.stack([pair(halved, v) for v in ys]))
    d4 = stacked(np.stack([pair(v, halved) for v in ys]))
    d5 = stacked(np.stack([pair(v, freq) for v in xs]))
    mask = np.zeros((4, 40, 128), np.float32)
    spread = np.zeros((128, 512))
    order = np.zeros((512, 512))
    for c in range(C):
        mask[c // 9, c, (c % 9) * MZ : (c % 9) * MZ + MZ] = 1
    for c in range(9):
        for k in range(MZ):
            spread[c * MZ + k, k * C : k * C + C] = 1
    for k in range(MZ):
        for o in range(C):
            order[k * C + o, (o // 9) * 128 + (o % 9) * MZ + k] = 1
    return (
        np.stack(halves(forward)),
        d1,
        d2,
        d4,
        d5,
        mask,
        spread.astype(jnp.bfloat16),
        order.astype(jnp.bfloat16),
        np.stack(halves(backward), axis=1),
    )


def split(value):
    high = value.astype(BF16)
    low = (value - high.astype(F32)).astype(BF16)
    return high, low


def split32(value):
    high = value.astype(BF16).astype(F32)
    return high, value - high


def dot(left, right):
    return jnp.dot(left, right, preferred_element_type=F32)


def gelu(value):
    return 0.5 * value * (1.0 + lax.erf(value * 0.7071067811865476))


def kernel(
    state_hbm, wf_hbm, ws_hbm, sr_hbm, si_hbm,
    fz_hbm, d1_hbm, d2_hbm, d4_hbm, d5_hbm, mk_hbm, ex_hbm, pm_hbm, fi_hbm,
    out_ref,
    st, wf, ws, sr, si, fz, d1, d2, d4, d5, mk, ex, pm, fi,
    s1, r1, s2, r2, s3, r3, s4, r4, s5, r5, s6, r6,
    tt, m8, wst1, wst2, cc, stage, ubh, ubl, hid, stage2, ub2h, ub2l, ct, n2, co,
    load_sem, send_sem, recv_sem, halo_send, halo_recv, ready_sem,
):
    i = lax.axis_index("gx")
    j = lax.axis_index("gy")
    g = (i % 8) // 2
    l = (i // 8) * 2 + i % 2
    yy = j // 4
    zz = j % 4

    sources = [
        (state_hbm, st), (fz_hbm, fz), (d1_hbm.at[g], d1), (d2_hbm.at[zz], d2), (wf_hbm, wf),
        (ws_hbm, ws), (sr_hbm, sr), (si_hbm, si), (mk_hbm, mk), (ex_hbm, ex),
        (pm_hbm, pm), (d4_hbm.at[zz], d4), (d5_hbm.at[g], d5), (fi_hbm, fi),
    ]
    loads = [pltpu.make_async_copy(src, dst, load_sem.at[n]) for n, (src, dst) in enumerate(sources)]
    loads[0].start()
    loads[1].start()
    (l_st, l_fz, l_d1, l_d2, l_wf, l_ws, l_sr, l_si, l_mk, l_ex, l_pm, l_d4, l_d5, l_fi) = loads

    def peer(t, y):
        return ((t // 2) * 8 + g * 2 + t % 2, y * 4 + zz)

    barrier = pltpu.get_barrier_semaphore()

    across = [(i, yy * 4 + (zz + 1) % 4), (i, yy * 4 + (zz + 3) % 4)]
    for device in across:
        pl.semaphore_signal(barrier, inc=1, device_id=device, device_id_type=MESH)

    above = (zz == 3) & (j < GY - 1)
    below = (zz == 0) & (j > 0)

    @pl.when(above)
    def _():
        pl.semaphore_signal(barrier, inc=1, device_id=(i, (j + 1) % GY), device_id_type=MESH)

    @pl.when(below)
    def _():
        pl.semaphore_signal(barrier, inc=1, device_id=(i, (j + GY - 1) % GY), device_id_type=MESH)

    for n in range(1, 4):
        along = (i // 8) * 8 + ((g + n) % 4) * 2 + i % 2
        pl.semaphore_signal(barrier, inc=1, device_id=(along, j), device_id_type=MESH)

    @pl.loop(1, GROUP)
    def _(s):
        for n in range(4):
            pl.semaphore_signal(
                barrier, inc=1, device_id=peer((l + s) % GROUP, (yy + n) % 4), device_id_type=MESH
            )

    for n in range(1, 4):
        pl.semaphore_signal(barrier, inc=1, device_id=peer(l, (yy + n) % 4), device_id_type=MESH)


    def remote(src, dst, stage_no, device):
        return pltpu.make_async_remote_copy(
            src_ref=src, dst_ref=dst, send_sem=send_sem.at[stage_no], recv_sem=recv_sem.at[stage_no],
            device_id=device, device_id_type=MESH,
        )

    def rows(start, size):
        return pl.ds(pl.multiple_of(start, 8), size)

    def wait_recv(buffer, count, stage_no):
        part = buffer.at[pl.ds(0, count)]
        pltpu.make_async_copy(part, part, recv_sem.at[stage_no]).wait()

    def wait_send(buffer, count, stage_no):
        part = buffer.at[pl.ds(0, count)]
        pltpu.make_async_copy(part, part, send_sem.at[stage_no]).wait()

    lane = lax.broadcasted_iota(jnp.int32, (1, 128), 1)
    first_half = lane < 64

    l_st.wait()
    l_fz.wait()
    field = st[...].reshape(NX * NY, C * Z)
    for e in range(2):
        left = jnp.concatenate([field[:, h * 1152 + e * 512 : h * 1152 + e * 512 + 640] for h in range(2)], axis=0)
        high, low = split(left)
        fh = fz[0, 64 * (1 - e) : 64 * (1 - e) + 640, :]
        fl = fz[1, 64 * (1 - e) : 64 * (1 - e) + 640, :]
        res = dot(high, fh) + dot(low, fh) + dot(high, fl)
        for h in range(2):
            for part in range(2):
                for x in range(NX):
                    s1[pl.ds((2 * h + e) * 64 + x * 2 + part, 8, stride=8), :] = res[
                        h * 32 + x * 8 : h * 32 + x * 8 + 8, part * 128 : part * 128 + 128
                    ]
    cc[...] = jnp.zeros_like(cc)
    t2 = tt.reshape(8 * 12 * 24, 128)
    for x in range(NX):
        for m in range(18):
            t2[pl.ds(((x + 2) * 12 + 2) * 24 + m, 8, stride=24), :] = st[x, :, m * 128 : (m + 1) * 128]

    near = 31 + 3 + 2
    pl.semaphore_wait(barrier, jnp.where(above | below, near + 1, near))
    def halo(n, src, dst, device):
        return pltpu.make_async_remote_copy(
            src_ref=src, dst_ref=dst, send_sem=halo_send.at[n], recv_sem=halo_recv.at[n],
            device_id=device, device_id_type=MESH,
        )

    down_y = halo(0, tt.at[2:6, 2:4], tt.at[2:6, 10:12], (i, (j + GY - 1) % GY))
    up_y = halo(1, tt.at[2:6, 8:10], tt.at[2:6, 0:2], (i, (j + 1) % GY))
    down_x = halo(2, tt.at[2:4], tt.at[6:8], ((i + GX - 1) % GX, j))
    up_x = halo(3, tt.at[4:6], tt.at[0:2], ((i + 1) % GX, j))

    @pl.when(j > 0)
    def _():
        down_y.start()

    @pl.when(j < GY - 1)
    def _():
        up_y.start()

    slot = yy * 8 + l

    @pl.loop(1, 32)
    def _(s):
        n = (slot + s) % 32
        remote(s1.at[rows(n * 8, 8)], r1.at[rows(slot * 8, 8)], 0, peer(n % 8, n // 8)).start()

    r1[rows(slot * 8, 8), :] = s1[rows(slot * 8, 8), :]
    for load in loads[2:]:
        load.start()

    @pl.when(j == 0)
    def _():
        tt[2:6, 0:2] = jnp.zeros((4, 2, 24, 128), F32)

    @pl.when(j == GY - 1)
    def _():
        tt[2:6, 10:12] = jnp.zeros((4, 2, 24, 128), F32)

    @pl.when(i == 0)
    def _():
        tt[0:2] = jnp.zeros((2, 12, 24, 128), F32)

    @pl.when(i == GX - 1)
    def _():
        tt[6:8] = jnp.zeros((2, 12, 24, 128), F32)

    def filters(src, scratch):
        scratch[...] = jnp.zeros_like(scratch)
        for tap_x in range(3):
            for tap_y in range(3):
                tap = tap_x * 3 + tap_y
                high, low = split32(src[tap_x, tap_y])
                scratch[0:36, tap * KB : tap * KB + 108] = high
                scratch[40:76, tap * KB : tap * KB + 108] = low

    l_wf.wait()
    filters(wf, wst1)

    wait_recv(r1, 31 * 8, 0)
    for device in across:
        pl.semaphore_signal(ready_sem, inc=1, device_id=device, device_id_type=MESH)
    l_d1.wait()

    def gathered(buffer):
        return jnp.concatenate([buffer[pl.ds(k, 32, stride=8), :] for k in range(8)], axis=1)

    def tripled(value):
        high, low = split(value)
        return jnp.concatenate([high, low, high], axis=0)

    def exchanged(buffer):
        return jnp.concatenate(
            [buffer[pl.ds(y * 64 + part, 32, stride=2), :] for part in range(2) for y in range(4)], axis=1
        )

    def combine(res, sign):
        half = res.shape[1] // 2
        top, bottom = res[:32], res[32:]
        real = top[:, :half] + sign * bottom[:, half:]
        imag = top[:, half:] - sign * bottom[:, :half]
        return real, imag

    real, imag = combine(dot(d1[...], tripled(exchanged(r1))), 1.0)
    for k in range(4):
        s2[pl.ds(k, 32, stride=8), :] = real[:, k * 128 : k * 128 + 128]
        s2[pl.ds(k + 4, 32, stride=8), :] = imag[:, k * 128 : k * 128 + 128]

    @pl.loop(1, GX)
    def _(s):
        t = (i + s) % GX
        remote(s2.at[rows(t * 8, 8)], r2.at[rows((g * 8 + l) * 8, 8)], 1, (t, j)).start()

    r2[rows((g * 8 + l) * 8, 8), :] = s2[rows(i * 8, 8), :]
    l_ws.wait()
    filters(ws, wst2)

    wait_recv(r2, 31 * 8, 1)
    l_d2.wait()
    parts = []
    for part in range(2):
        column = []
        for y in range(4):
            k = part * 4 + y
            terms = [r2[pl.ds(n * 64 + k, 8, stride=8), :] for n in range(4)]
            column.append((terms[0] + terms[1]) + (terms[2] + terms[3]))
        parts.append(jnp.concatenate(column, axis=0))
    result = combine(dot(d2[...], tripled(jnp.concatenate(parts, axis=1))), 1.0)
    for b in range(2):
        for part in range(2):
            s3[:, b * 2 + part, :] = result[part][b * 16 : b * 16 + 16]

    pl.semaphore_wait(ready_sem, 2)

    @pl.loop(1, GY)
    def _(s):
        t = (j + s) % GY
        remote(s3.at[t], r3.at[j], 2, (i, t)).start()

    r3[j] = s3[j]

    @pl.when(j > 0)
    def _():
        up_y.wait_recv()

    @pl.when(j < GY - 1)
    def _():
        down_y.wait_recv()

    @pl.when(i > 0)
    def _():
        down_x.start()

    @pl.when(i < GX - 1)
    def _():
        up_x.start()

    wait_recv(r3, GY - 1, 2)
    total = [(r3[4 * n] + r3[4 * n + 1]) + (r3[4 * n + 2] + r3[4 * n + 3]) for n in range(4)]
    for load in (l_mk, l_ex, l_sr, l_si, l_pm):
        load.wait()
    placed = []
    for q in range(2):
        for part in range(2):
            acc = None
            for cg in range(4):
                n = q * 2 + part
                term = total[cg][n : n + 1, :] * mk[cg]
                acc = term if acc is None else acc + term
            placed.append(acc)
    high, low = split(jnp.concatenate(placed, axis=0))
    wide = dot(high, ex[...]) + dot(low, ex[...])
    m8[...] = jnp.zeros_like(m8)
    for q in range(2):
        c_re = wide[q * 80 : q * 80 + 36, :432]
        c_im = wide[q * 80 + 40 : q * 80 + 76, :432]
        w_re, w_im = sr[:, q, :], si[:, q, :]
        m8[2 * q : 2 * q + 1, 0:432] = jnp.sum(c_re * w_re - c_im * w_im, axis=0, keepdims=True)
        m8[2 * q + 1 : 2 * q + 2, 0:432] = jnp.sum(c_re * w_im + c_im * w_re, axis=0, keepdims=True)
    high, low = split32(m8[...])
    moved = dot(jnp.concatenate([high, low], axis=0).astype(BF16), pm[...])
    mixed = moved[0:8] + moved[8:16]
    for cg in range(4):
        s4[cg] = mixed[0:4, cg * 128 : cg * 128 + 128]

    @pl.loop(1, GY)
    def _(s):
        t = (j + s) % GY
        remote(s4.at[t // 4], r4.at[j], 3, (i, t)).start()

    r4[j] = s4[yy]

    @pl.when(i > 0)
    def _():
        up_x.wait_recv()

    @pl.when(i < GX - 1)
    def _():
        down_x.wait_recv()

    z_of = lane % 64

    def shifted(value, d):
        if d == 0:
            return jnp.where(z_of == 0, 0.0, pltpu.roll(value, 1, axis=1))
        if d == 2:
            return jnp.where(z_of == 63, 0.0, pltpu.roll(value, 127, axis=1))
        return value

    def columns(value, buffer, base):
        for d in range(3):
            buffer[base + d * 36 : base + d * 36 + 36, :] = shifted(value, d)[0:36]
        return split(buffer[base : base + KB, :])

    stage[...] = jnp.zeros_like(stage)
    stage2[...] = jnp.zeros_like(stage2)

    @pl.loop(0, 8)
    def _(x):
        for u in range(7):
            near = t2[rows((x * 12 + u) * 24, 24), :]
            far = t2[rows((x * 12 + u + 5) * 24, 24), :]
            even = jnp.where(first_half, near, pltpu.roll(far, 64, axis=1))
            odd = jnp.where(first_half, pltpu.roll(near, 64, axis=1), far)
            cc[pl.ds(u * 40, 18, stride=2), :] = even[0:18]
            cc[pl.ds(u * 40 + 1, 18, stride=2), :] = odd[0:18]
            high, low = columns(cc[u * 40 : u * 40 + 40, :], stage, u * KB)
            for b in range(3):
                v = u - b
                if 0 <= v < 5:
                    place = pl.ds(pl.multiple_of(x * 336 + b * KB, 16), KB)
                    ubh[place, v * 128 : v * 128 + 128] = high
                    ubl[place, v * 128 : v * 128 + 128] = low

    w1 = wst1[...].astype(BF16)
    wide_lane = lax.broadcasted_iota(jnp.int32, (1, 640), 1)
    keep_y = jnp.where((wide_lane < 64) & (j == 0), 0.0, 1.0) * jnp.where(
        (wide_lane >= 576) & (j == GY - 1), 0.0, 1.0
    )

    @pl.loop(0, 6)
    def _(x):
        place = pl.ds(pl.multiple_of(x * 336, 16), 1008)
        res = dot(w1, ubh[place, :])
        value = res[0:40] + res[40:80] + dot(w1[0:40], ubl[place, :])
        outside = ((x == 0) & (i == 0)) | ((x == 5) & (i == GX - 1))
        keep = keep_y * jnp.where(outside, 0.0, 1.0)
        hid[rows(x * 40, 40), :] = gelu(value) * keep

    wait_recv(r4, GY - 1, 3)
    l_d4.wait()
    modes = jnp.concatenate(
        [jnp.concatenate([r4[:, b * 2 + part, :] for b in range(2)], axis=0) for part in range(2)], axis=1
    )
    result = combine(dot(d4[...], tripled(modes)), -1.0)
    for part in range(2):
        for y in range(4):
            s5[pl.ds(part * 4 + y, 8, stride=8), :] = result[part][y * 8 : y * 8 + 8]

    @pl.loop(1, GX)
    def _(s):
        t = (i + s) % GX
        row = (t // 8) * 2 + t % 2
        remote(s5.at[rows(row * 8, 8)], r5.at[rows(i * 8, 8)], 4, (t, j)).start()

    r5[rows(i * 8, 8), :] = s5[rows(l * 8, 8), :]

    @pl.loop(0, 6)
    def _(x):
        pairs = [hid[rows(x * 40, 40), v * 128 : v * 128 + 128] for v in range(5)]
        units = [(pairs[n], [(b, n - b) for b in range(3) if 0 <= n - b < 3]) for n in range(5)]
        units.append((jnp.where(first_half, pairs[3], pltpu.roll(pairs[4], 64, axis=1)), [(0, 3)]))
        units.append((jnp.where(first_half, pairs[4], pairs[0]), [(1, 3)]))
        units.append((jnp.where(first_half, pltpu.roll(pairs[0], 64, axis=1), pairs[1]), [(2, 3)]))
        for n, (value, places) in enumerate(units):
            high, low = columns(value, stage2, n * KB)
            for b, v in places:
                place = pl.ds(pl.multiple_of(x * 336 + b * KB, 16), KB)
                ub2h[place, v * 128 : v * 128 + 128] = high
                ub2l[place, v * 128 : v * 128 + 128] = low

    wait_recv(r5, 31 * 8, 4)
    l_d5.wait()
    result = combine(dot(d5[...], tripled(gathered(r5))), -1.0)
    for part in range(2):
        for y in range(4):
            s6[pl.ds(y * 64 + part, 32, stride=2), :] = result[part][:, y * 128 : y * 128 + 128]

    @pl.loop(1, 32)
    def _(s):
        n = (slot + s) % 32
        remote(s6.at[rows(n * 8, 8)], r6.at[rows(slot * 8, 8)], 5, peer(n % 8, n // 8)).start()

    r6[rows(slot * 8, 8), :] = s6[rows(slot * 8, 8), :]

    w2 = wst2[...].astype(BF16)

    @pl.loop(0, NX)
    def _(x):
        place = pl.ds(pl.multiple_of(x * 336, 16), 1008)
        res = dot(w2, ub2h[place, :])
        value = res[0:40] + res[40:80] + dot(w2[0:40], ub2l[place, :])
        for v in range(4):
            ct[v * 40 : v * 40 + 40, :] = value[:, v * 128 : v * 128 + 128]
        for v in range(4):
            even = ct[pl.ds(v * 40, 18, stride=2), :]
            odd = ct[pl.ds(v * 40 + 1, 18, stride=2), :]
            near = jnp.where(first_half, even, pltpu.roll(odd, 64, axis=1))
            far = jnp.where(first_half, pltpu.roll(even, 64, axis=1), odd)
            y_near, y_far = (v, v + 5) if v < 3 else (3, 4)
            n2[y_near * 24 : y_near * 24 + 18, :] = near
            n2[y_far * 24 : y_far * 24 + 18, :] = far
        for m in range(18):
            co[rows(x * 8, 8), m * 128 : m * 128 + 128] = n2[pl.ds(m, 8, stride=24), :]

    wait_recv(r6, 31 * 8, 5)
    l_fi.wait()
    results = []
    for e in range(2):
        left = jnp.concatenate(
            [
                jnp.concatenate(
                    [
                        jnp.concatenate(
                            [r6[pl.ds((2 * h + e) * 64 + x * 2 + part, 8, stride=8), :] for x in range(NX)], axis=0
                        )
                        for part in range(2)
                    ],
                    axis=1,
                )
                for h in range(2)
            ],
            axis=0,
        )
        high, low = split(left)
        results.append(dot(high, fi[e, 0]) + dot(low, fi[e, 0]) + dot(high, fi[e, 1]))
    for h in range(2):
        one, two = results[0][h * 32 : h * 32 + 32], results[1][h * 32 : h * 32 + 32]
        spectral = jnp.concatenate([one[:, :512], one[:, 512:] + two[:, :128], two[:, 128:]], axis=1)
        full = spectral + co[:, h * 1152 : h * 1152 + 1152]
        for x in range(NX):
            out_ref[x, :, h * 1152 : h * 1152 + 1152] = full[x * 8 : x * 8 + 8]

    wait_send(s1, 31 * 8, 0)
    wait_send(s2, 31 * 8, 1)
    wait_send(r3, GY - 1, 2)
    wait_send(r4, GY - 1, 3)
    wait_send(r5, 31 * 8, 4)
    wait_send(s6, 31 * 8, 5)

    @pl.when(j > 0)
    def _():
        down_y.wait_send()

    @pl.when(j < GY - 1)
    def _():
        up_y.wait_send()

    @pl.when(i > 0)
    def _():
        down_x.wait_send()

    @pl.when(i < GX - 1)
    def _():
        up_x.wait_send()


def on_device(state_field, conv_first, conv_second, spec_real, spec_imag):
    constants = [jnp.asarray(t) for t in tables()]
    vm = pltpu.VMEM
    scratch = [
        vm((NX, NY, C * Z), F32), vm((3, 3, C, 3 * C), F32), vm((3, 3, C, 3 * C), F32),
        vm((C, 2, MZ * C), F32), vm((C, 2, MZ * C), F32),
        vm((2, 704, 256), BF16), vm((64, 96), BF16), vm((64, 96), BF16), vm((64, 96), BF16), vm((64, 96), BF16),
        vm((4, 40, 128), F32), vm((128, 512), BF16), vm((512, 512), BF16), vm((2, 2, 256, 640), BF16),
        vm((256, 128), F32), vm((256, 128), F32), vm((256, 128), F32), vm((256, 128), F32),
        vm((GY, 4, 128), F32), vm((GY, 4, 128), F32), vm((4, 4, 128), F32), vm((GY, 4, 128), F32),
        vm((64, 128), F32), vm((256, 128), F32), vm((256, 128), F32), vm((256, 128), F32),
        vm((8, 12, 24, 128), F32), vm((8, 512), F32), vm((80, 9 * KB), F32), vm((80, 9 * KB), F32),
        vm((280, 128), F32), vm((7 * KB, 128), F32), vm((8 * 336, 640), BF16), vm((8 * 336, 640), BF16),
        vm((240, 640), F32), vm((8 * KB, 128), F32), vm((6 * 336, 512), BF16), vm((6 * 336, 512), BF16),
        vm((160, 128), F32), vm((192, 128), F32), vm((32, C * Z), F32),
        pltpu.SemaphoreType.DMA((14,)), pltpu.SemaphoreType.DMA((6,)), pltpu.SemaphoreType.DMA((6,)),
        pltpu.SemaphoreType.DMA((4,)), pltpu.SemaphoreType.DMA((4,)), pltpu.SemaphoreType.REGULAR,
    ]
    before = pl.pallas_call(
        kernel,
        out_shape=jax.ShapeDtypeStruct((NX, NY, C * Z), F32),
        in_specs=[pl.BlockSpec(memory_space=pl.ANY)] * (5 + len(constants)),
        out_specs=pl.BlockSpec(memory_space=pltpu.VMEM),
        scratch_shapes=scratch,
        compiler_params=pltpu.CompilerParams(
            collective_id=0, has_side_effects=True, vmem_limit_bytes=56 * 1024 * 1024
        ),
    )(
        state_field, conv_first, conv_second,
        jnp.transpose(spec_real[0], (1, 0, 2)), jnp.transpose(spec_imag[0], (1, 0, 2)), *constants
    )
    return jax.nn.gelu(before, approximate=False)


def solution(mesh):
    in_specs = (P("gx", "gy", None), P(), P(), P("gx", "gy", None, None), P("gx", "gy", None, None))
    return jax.shard_map(
        on_device, mesh=mesh, in_specs=in_specs, out_specs=P("gx", "gy", None), check_vma=False
    )
```

```python
import jax
import jax.numpy as jnp
import numpy as np
from jax import lax
from jax.experimental import pallas as pl
from jax.experimental.pallas import tpu as pltpu
from jax.sharding import PartitionSpec as P

C = 36
Z = 64
MZ = 12
X = 128
Y = 128
GX = 32
GY = 16
NX = 4
NY = 8
GROUP = 8
KB = 112
F32 = jnp.float32
BF16 = jnp.bfloat16
MESH = pl.DeviceIdType.MESH


def halves(table):
    high = table.astype(jnp.bfloat16)
    low = (table - high.astype(np.float64)).astype(jnp.bfloat16)
    return high, low


def stacked(table):
    high, low = halves(table)
    return np.concatenate([high, high, low], axis=-1)


def tables():
    r = np.arange(MZ)
    z = np.arange(Z)
    zr = 2 * np.pi * np.outer(z, r) / Z
    forward = np.zeros((704, 256))
    backward = np.zeros((2, 256, 640))
    weight = np.where(r == 0, 1.0, 2.0) / (X * Y * Z)
    for c in range(9):
        rows = slice(64 + c * Z, 64 + c * Z + Z)
        forward[rows, c * MZ : c * MZ + MZ] = np.cos(zr)
        forward[rows, 128 + c * MZ : 128 + c * MZ + MZ] = -np.sin(zr)
        for e in range(2):
            cols = slice(64 * e + c * Z, 64 * e + c * Z + Z)
            backward[e, c * MZ : c * MZ + MZ, cols] = (np.cos(zr) * weight).T
            backward[e, 128 + c * MZ : 128 + c * MZ + MZ, cols] = -(np.sin(zr) * weight).T
    freq = np.where(np.arange(32) < 16, np.arange(32), np.arange(32) + 96)

    def pair(first, second):
        angle = 2 * np.pi * (np.outer(first, second) % 128) / 128
        return np.concatenate([np.cos(angle), np.sin(angle)], axis=0)

    members = np.array([[(t // 2) * 8 + g * 2 + t % 2 for t in range(GROUP)] for g in range(4)])
    xs = [(members[g][:, None] * NX + np.arange(NX)[None, :]).reshape(32) for g in range(4)]
    blocks = np.arange(4) * 4
    ys = [((blocks[:, None] + g) * NY + np.arange(NY)[None, :]).reshape(32) for g in range(4)]
    halved = np.concatenate([freq[0::2], freq[1::2]])
    d1 = stacked(np.stack([pair(freq, v) for v in xs]))
    d2 = stacked(np.stack([pair(halved, v) for v in ys]))
    d4 = stacked(np.stack([pair(v, halved) for v in ys]))
    d5 = stacked(np.stack([pair(v, freq) for v in xs]))
    mask = np.zeros((4, 40, 128), np.float32)
    spread = np.zeros((128, 512))
    order = np.zeros((512, 512))
    for c in range(C):
        mask[c // 9, c, (c % 9) * MZ : (c % 9) * MZ + MZ] = 1
    for c in range(9):
        for k in range(MZ):
            spread[c * MZ + k, k * C : k * C + C] = 1
    for k in range(MZ):
        for o in range(C):
            order[k * C + o, (o // 9) * 128 + (o % 9) * MZ + k] = 1
    return (
        np.stack(halves(forward)),
        d1,
        d2,
        d4,
        d5,
        mask,
        spread.astype(jnp.bfloat16),
        order.astype(jnp.bfloat16),
        np.stack(halves(backward), axis=1),
    )


def split(value):
    high = value.astype(BF16)
    low = (value - high.astype(F32)).astype(BF16)
    return high, low


def split32(value):
    high = value.astype(BF16).astype(F32)
    return high, value - high


def dot(left, right):
    return jnp.dot(left, right, preferred_element_type=F32)


def gelu(value):
    return 0.5 * value * (1.0 + lax.erf(value * 0.7071067811865476))


def kernel(
    state_hbm, wf_hbm, ws_hbm, sr_hbm, si_hbm,
    fz_hbm, d1_hbm, d2_hbm, d4_hbm, d5_hbm, mk_hbm, ex_hbm, pm_hbm, fi_hbm,
    out_ref,
    st, wf, ws, sr, si, fz, d1, d2, d4, d5, mk, ex, pm, fi,
    s1, r1, s2, r2, s3, r3, s4, r4, s5, r5, s6, r6,
    tt, m8, wst1, wst2, cc, stage, ubh, ubl, hid, stage2, ub2h, ub2l, ct, n2, co,
    load_sem, send_sem, recv_sem, halo_send, halo_recv, ready_sem,
):
    i = lax.axis_index("gx")
    j = lax.axis_index("gy")
    g = (i % 8) // 2
    l = (i // 8) * 2 + i % 2
    yy = j // 4
    zz = j % 4

    sources = [
        (state_hbm, st), (fz_hbm, fz), (d1_hbm.at[g], d1), (d2_hbm.at[zz], d2), (wf_hbm, wf),
        (ws_hbm, ws), (sr_hbm, sr), (si_hbm, si), (mk_hbm, mk), (ex_hbm, ex),
        (pm_hbm, pm), (d4_hbm.at[zz], d4), (d5_hbm.at[g], d5), (fi_hbm, fi),
    ]
    loads = [pltpu.make_async_copy(src, dst, load_sem.at[n]) for n, (src, dst) in enumerate(sources)]
    loads[0].start()
    loads[1].start()
    (l_st, l_fz, l_d1, l_d2, l_wf, l_ws, l_sr, l_si, l_mk, l_ex, l_pm, l_d4, l_d5, l_fi) = loads

    def peer(t, y):
        return ((t // 2) * 8 + g * 2 + t % 2, y * 4 + zz)

    barrier = pltpu.get_barrier_semaphore()

    across = [(i, yy * 4 + (zz + 1) % 4), (i, yy * 4 + (zz + 3) % 4)]
    for device in across:
        pl.semaphore_signal(barrier, inc=1, device_id=device, device_id_type=MESH)

    above = (zz == 3) & (j < GY - 1)
    below = (zz == 0) & (j > 0)

    @pl.when(above)
    def _():
        pl.semaphore_signal(barrier, inc=1, device_id=(i, (j + 1) % GY), device_id_type=MESH)

    @pl.when(below)
    def _():
        pl.semaphore_signal(barrier, inc=1, device_id=(i, (j + GY - 1) % GY), device_id_type=MESH)

    for n in range(1, 4):
        along = (i // 8) * 8 + ((g + n) % 4) * 2 + i % 2
        pl.semaphore_signal(barrier, inc=1, device_id=(along, j), device_id_type=MESH)

    @pl.loop(1, GROUP)
    def _(s):
        for n in range(4):
            pl.semaphore_signal(
                barrier, inc=1, device_id=peer((l + s) % GROUP, (yy + n) % 4), device_id_type=MESH
            )

    for n in range(1, 4):
        pl.semaphore_signal(barrier, inc=1, device_id=peer(l, (yy + n) % 4), device_id_type=MESH)


    def remote(src, dst, stage_no, device):
        return pltpu.make_async_remote_copy(
            src_ref=src, dst_ref=dst, send_sem=send_sem.at[stage_no], recv_sem=recv_sem.at[stage_no],
            device_id=device, device_id_type=MESH,
        )

    def rows(start, size):
        return pl.ds(pl.multiple_of(start, 8), size)

    def wait_recv(buffer, count, stage_no):
        part = buffer.at[pl.ds(0, count)]
        pltpu.make_async_copy(part, part, recv_sem.at[stage_no]).wait()

    def wait_send(buffer, count, stage_no):
        part = buffer.at[pl.ds(0, count)]
        pltpu.make_async_copy(part, part, send_sem.at[stage_no]).wait()

    lane = lax.broadcasted_iota(jnp.int32, (1, 128), 1)
    first_half = lane < 64

    l_st.wait()
    l_fz.wait()
    field = st[...].reshape(NX * NY, C * Z)
    for e in range(2):
        left = jnp.concatenate([field[:, h * 1152 + e * 512 : h * 1152 + e * 512 + 640] for h in range(2)], axis=0)
        high, low = split(left)
        fh = fz[0, 64 * (1 - e) : 64 * (1 - e) + 640, :]
        fl = fz[1, 64 * (1 - e) : 64 * (1 - e) + 640, :]
        res = dot(high, fh) + dot(low, fh) + dot(high, fl)
        for h in range(2):
            for part in range(2):
                for x in range(NX):
                    s1[pl.ds((2 * h + e) * 64 + x * 2 + part, 8, stride=8), :] = res[
                        h * 32 + x * 8 : h * 32 + x * 8 + 8, part * 128 : part * 128 + 128
                    ]
    cc[...] = jnp.zeros_like(cc)
    t2 = tt.reshape(8 * 12 * 24, 128)
    for x in range(NX):
        for m in range(18):
            t2[pl.ds(((x + 2) * 12 + 2) * 24 + m, 8, stride=24), :] = st[x, :, m * 128 : (m + 1) * 128]

    near = 31 + 3 + 2
    pl.semaphore_wait(barrier, jnp.where(above | below, near + 1, near))
    def halo(n, src, dst, device):
        return pltpu.make_async_remote_copy(
            src_ref=src, dst_ref=dst, send_sem=halo_send.at[n], recv_sem=halo_recv.at[n],
            device_id=device, device_id_type=MESH,
        )

    down_y = halo(0, tt.at[2:6, 2:4], tt.at[2:6, 10:12], (i, (j + GY - 1) % GY))
    up_y = halo(1, tt.at[2:6, 8:10], tt.at[2:6, 0:2], (i, (j + 1) % GY))
    down_x = halo(2, tt.at[2:4], tt.at[6:8], ((i + GX - 1) % GX, j))
    up_x = halo(3, tt.at[4:6], tt.at[0:2], ((i + 1) % GX, j))

    @pl.when(j > 0)
    def _():
        down_y.start()

    @pl.when(j < GY - 1)
    def _():
        up_y.start()

    slot = yy * 8 + l

    @pl.loop(1, 32)
    def _(s):
        n = (slot + s) % 32
        remote(s1.at[rows(n * 8, 8)], r1.at[rows(slot * 8, 8)], 0, peer(n % 8, n // 8)).start()

    r1[rows(slot * 8, 8), :] = s1[rows(slot * 8, 8), :]
    for load in loads[2:]:
        load.start()

    @pl.when(j == 0)
    def _():
        tt[2:6, 0:2] = jnp.zeros((4, 2, 24, 128), F32)

    @pl.when(j == GY - 1)
    def _():
        tt[2:6, 10:12] = jnp.zeros((4, 2, 24, 128), F32)

    @pl.when(i == 0)
    def _():
        tt[0:2] = jnp.zeros((2, 12, 24, 128), F32)

    @pl.when(i == GX - 1)
    def _():
        tt[6:8] = jnp.zeros((2, 12, 24, 128), F32)

    def filters(src, scratch):
        scratch[...] = jnp.zeros_like(scratch)
        for tap_x in range(3):
            for tap_y in range(3):
                tap = tap_x * 3 + tap_y
                high, low = split32(src[tap_x, tap_y])
                scratch[0:36, tap * KB : tap * KB + 108] = high
                scratch[40:76, tap * KB : tap * KB + 108] = low

    l_wf.wait()
    filters(wf, wst1)

    wait_recv(r1, 31 * 8, 0)
    for device in across:
        pl.semaphore_signal(ready_sem, inc=1, device_id=device, device_id_type=MESH)
    l_d1.wait()

    def gathered(buffer):
        return jnp.concatenate([buffer[pl.ds(k, 32, stride=8), :] for k in range(8)], axis=1)

    def tripled(value):
        high, low = split(value)
        return jnp.concatenate([high, low, high], axis=0)

    def exchanged(buffer):
        return jnp.concatenate(
            [buffer[pl.ds(y * 64 + part, 32, stride=2), :] for part in range(2) for y in range(4)], axis=1
        )

    def combine(res, sign):
        half = res.shape[1] // 2
        top, bottom = res[:32], res[32:]
        real = top[:, :half] + sign * bottom[:, half:]
        imag = top[:, half:] - sign * bottom[:, :half]
        return real, imag

    real, imag = combine(dot(d1[...], tripled(exchanged(r1))), 1.0)
    for k in range(4):
        s2[pl.ds(k, 32, stride=8), :] = real[:, k * 128 : k * 128 + 128]
        s2[pl.ds(k + 4, 32, stride=8), :] = imag[:, k * 128 : k * 128 + 128]

    @pl.loop(1, GX)
    def _(s):
        t = (i + s) % GX
        remote(s2.at[rows(t * 8, 8)], r2.at[rows((g * 8 + l) * 8, 8)], 1, (t, j)).start()

    r2[rows((g * 8 + l) * 8, 8), :] = s2[rows(i * 8, 8), :]
    l_ws.wait()
    filters(ws, wst2)

    wait_recv(r2, 31 * 8, 1)
    l_d2.wait()
    parts = []
    for part in range(2):
        column = []
        for y in range(4):
            k = part * 4 + y
            terms = [r2[pl.ds(n * 64 + k, 8, stride=8), :] for n in range(4)]
            column.append((terms[0] + terms[1]) + (terms[2] + terms[3]))
        parts.append(jnp.concatenate(column, axis=0))
    result = combine(dot(d2[...], tripled(jnp.concatenate(parts, axis=1))), 1.0)
    for b in range(2):
        for part in range(2):
            s3[:, b * 2 + part, :] = result[part][b * 16 : b * 16 + 16]

    pl.semaphore_wait(ready_sem, 2)

    @pl.loop(1, GY)
    def _(s):
        t = (j + s) % GY
        remote(s3.at[t], r3.at[j], 2, (i, t)).start()

    r3[j] = s3[j]

    @pl.when(j > 0)
    def _():
        up_y.wait_recv()

    @pl.when(j < GY - 1)
    def _():
        down_y.wait_recv()

    @pl.when(i > 0)
    def _():
        down_x.start()

    @pl.when(i < GX - 1)
    def _():
        up_x.start()

    wait_recv(r3, GY - 1, 2)
    total = [(r3[4 * n] + r3[4 * n + 1]) + (r3[4 * n + 2] + r3[4 * n + 3]) for n in range(4)]
    for load in (l_mk, l_ex, l_sr, l_si, l_pm):
        load.wait()
    placed = []
    for q in range(2):
        for part in range(2):
            acc = None
            for cg in range(4):
                n = q * 2 + part
                term = total[cg][n : n + 1, :] * mk[cg]
                acc = term if acc is None else acc + term
            placed.append(acc)
    high, low = split(jnp.concatenate(placed, axis=0))
    wide = dot(high, ex[...]) + dot(low, ex[...])
    m8[...] = jnp.zeros_like(m8)
    for q in range(2):
        c_re = wide[q * 80 : q * 80 + 36, :432]
        c_im = wide[q * 80 + 40 : q * 80 + 76, :432]
        w_re, w_im = sr[:, q, :], si[:, q, :]
        m8[2 * q : 2 * q + 1, 0:432] = jnp.sum(c_re * w_re - c_im * w_im, axis=0, keepdims=True)
        m8[2 * q + 1 : 2 * q + 2, 0:432] = jnp.sum(c_re * w_im + c_im * w_re, axis=0, keepdims=True)
    high, low = split32(m8[...])
    moved = dot(jnp.concatenate([high, low], axis=0).astype(BF16), pm[...])
    mixed = moved[0:8] + moved[8:16]
    for cg in range(4):
        s4[cg] = mixed[0:4, cg * 128 : cg * 128 + 128]

    @pl.loop(1, GY)
    def _(s):
        t = (j + s) % GY
        remote(s4.at[t // 4], r4.at[j], 3, (i, t)).start()

    r4[j] = s4[yy]

    @pl.when(i > 0)
    def _():
        up_x.wait_recv()

    @pl.when(i < GX - 1)
    def _():
        down_x.wait_recv()

    z_of = lane % 64

    def shifted(value, d):
        if d == 0:
            return jnp.where(z_of == 0, 0.0, pltpu.roll(value, 1, axis=1))
        if d == 2:
            return jnp.where(z_of == 63, 0.0, pltpu.roll(value, 127, axis=1))
        return value

    def columns(value, buffer, base):
        for d in range(3):
            buffer[base + d * 36 : base + d * 36 + 36, :] = shifted(value, d)[0:36]
        return split(buffer[base : base + KB, :])

    stage[...] = jnp.zeros_like(stage)
    stage2[...] = jnp.zeros_like(stage2)

    @pl.loop(0, 8)
    def _(x):
        for u in range(7):
            near = t2[rows((x * 12 + u) * 24, 24), :]
            far = t2[rows((x * 12 + u + 5) * 24, 24), :]
            even = jnp.where(first_half, near, pltpu.roll(far, 64, axis=1))
            odd = jnp.where(first_half, pltpu.roll(near, 64, axis=1), far)
            cc[pl.ds(u * 40, 18, stride=2), :] = even[0:18]
            cc[pl.ds(u * 40 + 1, 18, stride=2), :] = odd[0:18]
            high, low = columns(cc[u * 40 : u * 40 + 40, :], stage, u * KB)
            for b in range(3):
                v = u - b
                if 0 <= v < 5:
                    place = pl.ds(pl.multiple_of(x * 336 + b * KB, 16), KB)
                    ubh[place, v * 128 : v * 128 + 128] = high
                    ubl[place, v * 128 : v * 128 + 128] = low

    w1 = wst1[...].astype(BF16)
    wide_lane = lax.broadcasted_iota(jnp.int32, (1, 640), 1)
    keep_y = jnp.where((wide_lane < 64) & (j == 0), 0.0, 1.0) * jnp.where(
        (wide_lane >= 576) & (j == GY - 1), 0.0, 1.0
    )

    @pl.loop(0, 6)
    def _(x):
        place = pl.ds(pl.multiple_of(x * 336, 16), 1008)
        res = dot(w1, ubh[place, :])
        value = res[0:40] + res[40:80] + dot(w1[0:40], ubl[place, :])
        outside = ((x == 0) & (i == 0)) | ((x == 5) & (i == GX - 1))
        keep = keep_y * jnp.where(outside, 0.0, 1.0)
        hid[rows(x * 40, 40), :] = gelu(value) * keep

    wait_recv(r4, GY - 1, 3)
    l_d4.wait()
    modes = jnp.concatenate(
        [jnp.concatenate([r4[:, b * 2 + part, :] for b in range(2)], axis=0) for part in range(2)], axis=1
    )
    result = combine(dot(d4[...], tripled(modes)), -1.0)
    for part in range(2):
        for y in range(4):
            s5[pl.ds(part * 4 + y, 8, stride=8), :] = result[part][y * 8 : y * 8 + 8]

    @pl.loop(1, GX)
    def _(s):
        t = (i + s) % GX
        row = (t // 8) * 2 + t % 2
        remote(s5.at[rows(row * 8, 8)], r5.at[rows(i * 8, 8)], 4, (t, j)).start()

    r5[rows(i * 8, 8), :] = s5[rows(l * 8, 8), :]

    @pl.loop(0, 6)
    def _(x):
        pairs = [hid[rows(x * 40, 40), v * 128 : v * 128 + 128] for v in range(5)]
        units = [(pairs[n], [(b, n - b) for b in range(3) if 0 <= n - b < 3]) for n in range(5)]
        units.append((jnp.where(first_half, pairs[3], pltpu.roll(pairs[4], 64, axis=1)), [(0, 3)]))
        units.append((jnp.where(first_half, pairs[4], pairs[0]), [(1, 3)]))
        units.append((jnp.where(first_half, pltpu.roll(pairs[0], 64, axis=1), pairs[1]), [(2, 3)]))
        for n, (value, places) in enumerate(units):
            high, low = columns(value, stage2, n * KB)
            for b, v in places:
                place = pl.ds(pl.multiple_of(x * 336 + b * KB, 16), KB)
                ub2h[place, v * 128 : v * 128 + 128] = high
                ub2l[place, v * 128 : v * 128 + 128] = low

    wait_recv(r5, 31 * 8, 4)
    l_d5.wait()
    result = combine(dot(d5[...], tripled(gathered(r5))), -1.0)
    for part in range(2):
        for y in range(4):
            s6[pl.ds(y * 64 + part, 32, stride=2), :] = result[part][:, y * 128 : y * 128 + 128]

    @pl.loop(1, 32)
    def _(s):
        n = (slot + s) % 32
        remote(s6.at[rows(n * 8, 8)], r6.at[rows(slot * 8, 8)], 5, peer(n % 8, n // 8)).start()

    r6[rows(slot * 8, 8), :] = s6[rows(slot * 8, 8), :]

    w2 = wst2[...].astype(BF16)

    @pl.loop(0, NX)
    def _(x):
        place = pl.ds(pl.multiple_of(x * 336, 16), 1008)
        res = dot(w2, ub2h[place, :])
        value = res[0:40] + res[40:80] + dot(w2[0:40], ub2l[place, :])
        for v in range(4):
            ct[v * 40 : v * 40 + 40, :] = value[:, v * 128 : v * 128 + 128]
        for v in range(4):
            even = ct[pl.ds(v * 40, 18, stride=2), :]
            odd = ct[pl.ds(v * 40 + 1, 18, stride=2), :]
            near = jnp.where(first_half, even, pltpu.roll(odd, 64, axis=1))
            far = jnp.where(first_half, pltpu.roll(even, 64, axis=1), odd)
            y_near, y_far = (v, v + 5) if v < 3 else (3, 4)
            n2[y_near * 24 : y_near * 24 + 18, :] = near
            n2[y_far * 24 : y_far * 24 + 18, :] = far
        for m in range(18):
            co[rows(x * 8, 8), m * 128 : m * 128 + 128] = n2[pl.ds(m, 8, stride=24), :]

    wait_recv(r6, 31 * 8, 5)
    l_fi.wait()
    results = []
    for e in range(2):
        left = jnp.concatenate(
            [
                jnp.concatenate(
                    [
                        jnp.concatenate(
                            [r6[pl.ds((2 * h + e) * 64 + x * 2 + part, 8, stride=8), :] for x in range(NX)], axis=0
                        )
                        for part in range(2)
                    ],
                    axis=1,
                )
                for h in range(2)
            ],
            axis=0,
        )
        high, low = split(left)
        results.append(dot(high, fi[e, 0]) + dot(low, fi[e, 0]) + dot(high, fi[e, 1]))
    for h in range(2):
        one, two = results[0][h * 32 : h * 32 + 32], results[1][h * 32 : h * 32 + 32]
        spectral = jnp.concatenate([one[:, :512], one[:, 512:] + two[:, :128], two[:, 128:]], axis=1)
        full = spectral + co[:, h * 1152 : h * 1152 + 1152]
        for x in range(NX):
            out_ref[x, :, h * 1152 : h * 1152 + 1152] = full[x * 8 : x * 8 + 8]

    wait_send(s1, 31 * 8, 0)
    wait_send(s2, 31 * 8, 1)
    wait_send(r3, GY - 1, 2)
    wait_send(r4, GY - 1, 3)
    wait_send(r5, 31 * 8, 4)
    wait_send(s6, 31 * 8, 5)

    @pl.when(j > 0)
    def _():
        down_y.wait_send()

    @pl.when(j < GY - 1)
    def _():
        up_y.wait_send()

    @pl.when(i > 0)
    def _():
        down_x.wait_send()

    @pl.when(i < GX - 1)
    def _():
        up_x.wait_send()


def on_device(state_field, conv_first, conv_second, spec_real, spec_imag):
    constants = [jnp.asarray(t) for t in tables()]
    vm = pltpu.VMEM
    scratch = [
        vm((NX, NY, C * Z), F32), vm((3, 3, C, 3 * C), F32), vm((3, 3, C, 3 * C), F32),
        vm((C, 2, MZ * C), F32), vm((C, 2, MZ * C), F32),
        vm((2, 704, 256), BF16), vm((64, 96), BF16), vm((64, 96), BF16), vm((64, 96), BF16), vm((64, 96), BF16),
        vm((4, 40, 128), F32), vm((128, 512), BF16), vm((512, 512), BF16), vm((2, 2, 256, 640), BF16),
        vm((256, 128), F32), vm((256, 128), F32), vm((256, 128), F32), vm((256, 128), F32),
        vm((GY, 4, 128), F32), vm((GY, 4, 128), F32), vm((4, 4, 128), F32), vm((GY, 4, 128), F32),
        vm((64, 128), F32), vm((256, 128), F32), vm((256, 128), F32), vm((256, 128), F32),
        vm((8, 12, 24, 128), F32), vm((8, 512), F32), vm((80, 9 * KB), F32), vm((80, 9 * KB), F32),
        vm((280, 128), F32), vm((7 * KB, 128), F32), vm((8 * 336, 640), BF16), vm((8 * 336, 640), BF16),
        vm((240, 640), F32), vm((8 * KB, 128), F32), vm((6 * 336, 512), BF16), vm((6 * 336, 512), BF16),
        vm((160, 128), F32), vm((192, 128), F32), vm((32, C * Z), F32),
        pltpu.SemaphoreType.DMA((14,)), pltpu.SemaphoreType.DMA((6,)), pltpu.SemaphoreType.DMA((6,)),
        pltpu.SemaphoreType.DMA((4,)), pltpu.SemaphoreType.DMA((4,)), pltpu.SemaphoreType.REGULAR,
    ]
    before = pl.pallas_call(
        kernel,
        out_shape=jax.ShapeDtypeStruct((NX, NY, C * Z), F32),
        in_specs=[pl.BlockSpec(memory_space=pl.ANY)] * (5 + len(constants)),
        out_specs=pl.BlockSpec(memory_space=pltpu.VMEM),
        scratch_shapes=scratch,
        compiler_params=pltpu.CompilerParams(
            collective_id=0, has_side_effects=True, vmem_limit_bytes=56 * 1024 * 1024
        ),
    )(
        state_field, conv_first, conv_second,
        jnp.transpose(spec_real[0], (1, 0, 2)), jnp.transpose(spec_imag[0], (1, 0, 2)), *constants
    )
    return gelu(before)


def solution(mesh):
    in_specs = (P("gx", "gy", None), P(), P(), P("gx", "gy", None, None), P("gx", "gy", None, None))
    return jax.shard_map(
        on_device, mesh=mesh, in_specs=in_specs, out_specs=P("gx", "gy", None), check_vma=False
    )
```
